32 devices in a mesh: row: 16 (over z, y, x), col: 2 (over core).
Axes of the slice: x: 2, y: 2, z: 4, core: 2. Of those that a mesh axis runs over, the one named last changes fastest.
Arguments:
- points: float32 [2048, 384], P(('row', 'col')), may hold values from -0.3 to 0.3
- coeffs: float32 [2048, 2], P(('row', 'col')), may hold values from -6 to 6
- metric: float32 [384, 384], replicated, may hold values from -1 to 5, as said below
Outputs:
- metric_next: float32 [384, 384], replicated
- transformed: float32 [2048, 384], P(('row', 'col'))
The draws below stay inside these ranges and needn't reach their ends.
Inputs may be any that keep to these rules, and one draw needn't show every extreme that they name: `metric`: symmetric and positive definite.
All inputs are finite; a program needn't handle non-finite values.
Results may differ from the reference program's by a relative error of at most 0.0003.
The reference program's roundings to bfloat16 on the way (of `mixed`) count: a program that leaves them out, or rounds other values in their place, can miss the bound.
Values sent between devices are 32-bit elements; how exact they have to be, the bound alone decides.
No kernel may reach another device: no remote copies, remote signals or barrier semaphores. Data moves between devices by JAX's collectives and lax.ppermute only.
A program may use at most 64 MiB of HBM per device.

```python
import math
import jax
import jax.numpy as jnp
from jax import lax

D = 384
C = 2
N = 2048


def draw_metric(key, part):
    key_base = jax.random.fold_in(key, 11)
    key_diag = jax.random.fold_in(key, 12)
    base = jax.random.normal(key_base, (D, D), jnp.float32)
    lower_log = jnp.log(0.5)
    upper_log = jnp.log(2.0)
    diag_vals = jnp.exp(jax.random.uniform(key_diag, (D,), jnp.float32, lower_log, upper_log))
    gram = jnp.dot(base, base.T, precision=jax.lax.Precision.HIGHEST) / (2.0 * D)
    return gram + jnp.diag(diag_vals)


def shard_levels(key, extent, shards, smallest, high):
    loudness = 1.0
    for position, shards_of in shards:
        heights = jax.random.uniform(jax.random.fold_in(jax.random.fold_in(key, 6), position), (shards_of,), jnp.float32, smallest / len(shards), high / len(shards))
        loudness = loudness * jnp.repeat(jnp.exp(heights), extent[position] // shards_of).reshape((-1,) + (1,) * (len(extent) - 1 - position))
    return loudness


def bell_draw(key, shape, scale, bound, cuts=(), dtype=jnp.bfloat16):
    drawn = jax.random.normal(key, shape, jnp.float32) * scale
    if len(cuts) > 0:
        drawn = shard_levels(key, shape, cuts, -0.22, 0.18) * drawn
    return jnp.clip(drawn, min=-bound, max=bound).astype(dtype)


def setup_inputs(seed: int = 0) -> dict:
    key_list = jax.random.split(jax.random.key(seed), 4)
    points = bell_draw(key_list[0], (N, D), 0.051, 0.3, ((0, 32),), jnp.float32)
    coeffs = bell_draw(key_list[1], (N, C), 1.0, 6.0, ((0, 32),), jnp.float32)
    metric = draw_metric(jax.random.fold_in(key_list[3], 71), 0)
    return dict(points=points, coeffs=coeffs, metric=metric)


HIGH = lax.Precision.HIGHEST

def tile_terms(query_y, query_norm, centers, center_coef, center_norm):
    cross_term = jnp.dot(query_y, centers.T, precision=HIGH, preferred_element_type=jnp.float32)
    dist_sq = query_norm[:, None] + center_norm[None, :] - 2.0 * cross_term
    distance = jnp.sqrt(jnp.maximum(dist_sq, 0.0))
    weights = jnp.exp(-distance) / jnp.maximum(distance, 0.5)
    coef_sums = jnp.dot(weights, center_coef, precision=HIGH, preferred_element_type=jnp.float32)
    mixed = (weights[:, None, :] * center_coef.T[None, :, :]).astype(jnp.bfloat16)
    rows_all = mixed.shape[0] * mixed.shape[1]
    center_sums = jnp.dot(mixed.reshape(rows_all, mixed.shape[2]), centers.astype(jnp.bfloat16), preferred_element_type=jnp.float32)
    return (coef_sums, center_sums.reshape(mixed.shape[0], mixed.shape[1], centers.shape[1]))

def reference(points, coeffs, metric):
    total = points.shape[0]
    width = points.shape[1]
    outs_n = coeffs.shape[1]
    mapped = jnp.dot(points, metric, precision=HIGH, preferred_element_type=jnp.float32)
    sqnorm = lax.optimization_barrier(jnp.sum(points * mapped, axis=1))
    qblock = math.gcd(total, 1024)
    cblock = math.gcd(total, 512)
    center_pts = points.reshape(total // cblock, cblock, width)
    center_cf = coeffs.reshape(total // cblock, cblock, outs_n)
    center_nm = sqnorm.reshape(total // cblock, cblock)

    def per_query(packed):
        query_x, query_y, query_n = packed

        def step(carry, cargs):
            coef_sums, center_sums = tile_terms(query_y, query_n, cargs[0], cargs[1], cargs[2])
            return ((carry[0] + coef_sums, carry[1] + center_sums), None)
        start = (jnp.zeros((qblock, outs_n), jnp.float32), jnp.zeros((qblock, outs_n, width), jnp.float32))
        (coef_sums, center_sums), _ = lax.scan(step, start, (center_pts, center_cf, center_nm))
        return coef_sums[:, :, None] * query_x[:, None, :] - center_sums
    partial_value = lax.map(per_query, (points.reshape(total // qblock, qblock, width), mapped.reshape(total // qblock, qblock, width), sqnorm.reshape(total // qblock, qblock)))
    grads = -jnp.dot(partial_value.reshape(total * outs_n, width), metric, precision=HIGH, preferred_element_type=jnp.float32)
    outer = lax.dot_general(grads, grads, (((0,), (0,)), ((), ())), precision=HIGH, preferred_element_type=jnp.float32)
    metric_next = outer * (width / jnp.trace(outer))
    transformed = jnp.dot(points, metric_next, precision=HIGH, preferred_element_type=jnp.float32)
    return (metric_next, transformed)
```

```python
import jax
import jax.numpy as jnp
from jax import lax
from jax.sharding import PartitionSpec as P

HIGH = lax.Precision.HIGHEST
AXES = ("row", "col")


def dot(a, b, dims=(((1,), (0,)), ((), ()))):
    return lax.dot_general(a, b, dims, precision=HIGH, preferred_element_type=jnp.float32)


def bits_of(count):
    assert count & (count - 1) == 0
    return [1 << b for b in range(count.bit_length() - 1)]


class Hops:
    def __init__(self, rows, cols):
        self.rows, self.cols = rows, cols

    def __call__(self, value, even, odd=None):
        odd = even if odd is None else odd
        pairs = []
        for r in range(self.rows):
            for c in range(self.cols):
                dr, dc = odd if c & 1 else even
                pairs.append((r * self.cols + c, (r ^ dr) * self.cols + (c ^ dc)))
        return lax.ppermute(value, AXES, pairs)


def pack_own(points, coeffs, metric):
    rows, width = points.shape
    norm = jnp.sum(points * dot(points, metric), axis=1)
    vals = jnp.concatenate([coeffs.T, norm[None, :]], axis=0)
    aux = jnp.pad(vals, ((0, 8 - vals.shape[0]), (0, width - rows)))
    return jnp.concatenate([points, aux], axis=0)


def tile_terms(query_x, metric, centers, coef, norm):
    query_y = dot(query_x, metric)
    query_n = jnp.sum(query_x * query_y, axis=1)
    cross = dot(query_y, centers, (((1,), (1,)), ((), ())))
    dist_sq = query_n[:, None] + norm[None, :] - 2.0 * cross
    distance = jnp.sqrt(jnp.maximum(dist_sq, 0.0))
    weights = jnp.exp(-distance) / jnp.maximum(distance, 0.5)
    low = centers.astype(jnp.bfloat16)
    parts = []
    for c in range(coef.shape[0]):
        scaled = weights * coef[c][None, :]
        sums = jnp.sum(scaled, axis=1)
        center_sums = jnp.dot(scaled.astype(jnp.bfloat16), low, preferred_element_type=jnp.float32)
        parts.append(sums[:, None] * query_x - center_sums)
    return jnp.concatenate(parts, axis=0)


def make_local(rows_all, cols_all):
    hop = Hops(rows_all, cols_all)
    row_bits = bits_of(rows_all)
    col_bits = bits_of(cols_all)
    bit_a, bit_b = row_bits[0], row_bits[1]
    line_bits = row_bits[2:]

    def gather_centers(block):
        have = [block]
        for bit in reversed(line_bits):
            have = have + [hop(piece, (bit, 0)) for piece in have]
        both = jnp.stack(have)
        for bit in col_bits:
            both = jnp.concatenate([both, hop(both, (0, bit))], axis=0)
        return both

    def local(points, coeffs, metric):
        own, width = points.shape
        outs_n = coeffs.shape[1]
        block = pack_own(points, coeffs, metric)
        got_a = hop(points, (bit_a, 0), (bit_b, 0))
        got_b = hop(jnp.concatenate([points, got_a], axis=0), (bit_b, 0), (bit_a, 0))
        held = gather_centers(block)
        count = held.shape[0]
        centers = held[:, :own].reshape(count * own, width)
        aux = held[:, own : own + outs_n + 1, :own].transpose(1, 0, 2).reshape(outs_n + 1, count * own)
        coef, norm = aux[:outs_n], aux[outs_n]

        away = jnp.concatenate([got_a, got_b[own:]], axis=0)
        home = jnp.concatenate([points, got_b[:own]], axis=0)
        sent = hop(tile_terms(away, metric, centers, coef, norm), (bit_a, 0), (bit_b, 0))
        total = (tile_terms(home, metric, centers, coef, norm) + sent).reshape(outs_n, 2, own, width)
        part = total[:, 0] + hop(total[:, 1], (bit_b, 0), (bit_a, 0))

        grads = dot(part.reshape(outs_n * own, width), metric)
        outer = dot(grads, grads, (((0,), (0,)), ((), ())))

        tile = 128 if width % 128 == 0 else width
        span = width // tile
        upper = [(i, j) for i in range(span) for j in range(i, span)]
        blocks = [outer[i * tile : (i + 1) * tile, j * tile : (j + 1) * tile] for i, j in upper]
        if len(blocks) % 2:
            blocks.append(jnp.zeros((tile, tile), jnp.float32))
        half = len(blocks) // 2
        first, second = jnp.stack(blocks[:half]), jnp.stack(blocks[half:])
        odd = (lax.axis_index("col") & 1) == 1
        keep = jnp.where(odd, second, first) + hop(jnp.where(odd, first, second), (0, 1))
        rest = [(bit, 0) for bit in row_bits]
        turn = len(rest) // 2
        for even_hop, odd_hop in zip(rest, rest[turn:] + rest[:turn]):
            keep = keep + hop(keep, even_hop, odd_hop)
        for bit in col_bits[1:]:
            keep = keep + hop(keep, (0, bit))
        other = hop(keep, (0, 1))
        first, second = jnp.where(odd, other, keep), jnp.where(odd, keep, other)
        final = dict(zip(upper, [first[k] for k in range(half)] + [second[k] for k in range(half)]))
        outer = jnp.concatenate(
            [
                jnp.concatenate([final[i, j] if i <= j else final[j, i].T for j in range(span)], axis=1)
                for i in range(span)
            ],
            axis=0,
        )
        metric_next = outer * (width / jnp.trace(outer))
        transformed = dot(points, metric_next)
        return (metric_next, transformed)

    return local


def solution(mesh):
    return jax.shard_map(
        make_local(mesh.shape["row"], mesh.shape["col"]),
        mesh=mesh,
        in_specs=(P(AXES, None), P(AXES, None), P()),
        out_specs=(P(), P(AXES, None)),
        check_vma=False,
    )
```

```python
import jax
import jax.numpy as jnp
from jax import lax
from jax.experimental import pallas as pl
from jax.experimental.pallas import tpu as pltpu
from jax.sharding import PartitionSpec as P

HIGH = lax.Precision.HIGHEST
AXES = ("row", "col")
EXTRA = 8


def dot(a, b, dims=(((1,), (0,)), ((), ()))):
    return lax.dot_general(a, b, dims, precision=HIGH, preferred_element_type=jnp.float32)


def bits_of(count):
    assert count & (count - 1) == 0
    return [1 << b for b in range(count.bit_length() - 1)]


def make_hop(rows, cols):
    def hop(value, even, odd=None):
        odd = even if odd is None else odd
        pairs = []
        for r in range(rows):
            for c in range(cols):
                dr, dc = odd if c & 1 else even
                pairs.append((r * cols + c, (r ^ dr) * cols + (c ^ dc)))
        return lax.ppermute(value, AXES, pairs)

    return hop


def call(body, out_shape, args, flops):
    moved = sum(4 * a.size for a in args) + sum(4 * s.size for s in jax.tree.leaves(out_shape))
    return pl.pallas_call(
        body,
        out_shape=out_shape,
        in_specs=[pl.BlockSpec(memory_space=pltpu.VMEM)] * len(args),
        out_specs=jax.tree.map(lambda _: pl.BlockSpec(memory_space=pltpu.VMEM), out_shape),
        compiler_params=pltpu.CompilerParams(vmem_limit_bytes=40 * 1024 * 1024),
        cost_estimate=pl.CostEstimate(flops=flops, bytes_accessed=moved, transcendentals=0),
    )(*args)


def shape(*dims):
    return jax.ShapeDtypeStruct(dims, jnp.float32)


def pack_own(points, coeffs):
    rows, width = points.shape
    cols = coeffs.T
    aux = jnp.concatenate([cols, cols], axis=1)
    aux = jnp.pad(aux, ((0, EXTRA - cols.shape[0]), (0, width - 2 * rows)))
    return jnp.concatenate([points, aux], axis=0)


def center_terms(refs, metric, own, outs_n):
    pieces, coefs = [], []
    for ref in refs:
        for k in range(ref.shape[0] // (own + EXTRA)):
            first = k * (own + EXTRA)
            pieces.append(ref[first : first + own, :])
            coefs.append(ref[first + own : first + own + EXTRA, 0 : 2 * own])
    centers = jnp.concatenate(pieces, axis=0)
    ones = jnp.ones((8, centers.shape[1]), jnp.float32)
    norm = dot(ones, centers * dot(centers, metric), (((1,), (1,)), ((), ())))[0:1]
    lane = lax.broadcasted_iota(jnp.int32, coefs[0].shape, 1)
    merged = [jnp.where(lane < own, coefs[k], coefs[k + 1]) for k in range(0, len(coefs), 2)]
    coef = jnp.concatenate(merged, axis=1)
    return centers, norm, [coef[c : c + 1] for c in range(outs_n)]


def query_sums(query_x, query_y, centers, norm, coefs):
    query_n = jnp.sum(query_x * query_y, axis=1, keepdims=True)
    cross = dot(query_y, centers, (((1,), (1,)), ((), ())))
    distance = jnp.sqrt(jnp.maximum(query_n + norm - 2.0 * cross, 0.0))
    weights = jnp.exp(-distance) / jnp.maximum(distance, 0.5)
    low = centers.astype(jnp.bfloat16)
    parts = []
    for coef in coefs:
        scaled = weights * coef
        sums = jnp.sum(scaled, axis=1, keepdims=True)
        center_sums = jnp.dot(scaled.astype(jnp.bfloat16), low, preferred_element_type=jnp.float32)
        parts.append(sums * query_x - center_sums)
    return parts


def early_sums(queries, blocks, metric, outs_n):
    own, width = queries[0].shape
    count = len(queries)

    def body(*refs):
        query_refs, block_refs = refs[:count], refs[count : count + len(blocks)]
        metric_ref, total_ref, mapped_ref = refs[count + len(blocks) :]
        query_x = jnp.concatenate([ref[...] for ref in query_refs], axis=0)
        query_y = dot(query_x, metric_ref[...])
        mapped_ref[...] = query_y
        for k in range(0, len(blocks), 2):
            parts = query_sums(query_x, query_y, *center_terms(block_refs[k : k + 2], metric_ref[...], own, outs_n))
            for c in range(outs_n):
                if k == 0:
                    total_ref[c] = parts[c]
                else:
                    total_ref[c] = total_ref[c] + parts[c]

    args = list(queries) + list(blocks) + [metric]
    centers = sum(b.shape[0] for b in blocks)
    flops = 12 * (count * own + centers) * width * width + 12 * count * own * centers * width
    return call(body, (shape(outs_n, count * own, width), shape(count * own, width)), args, flops)


def late_sums(queries, first, total, mapped, blocks, metric, outs_n):
    own, width = queries[0].shape
    count = len(queries)

    def body(*refs):
        query_refs, block_refs = refs[:count], refs[count : count + len(blocks)]
        metric_ref, total_ref, mapped_ref = refs[count + len(blocks) : count + len(blocks) + 3]
        out_refs = refs[count + len(blocks) + 3 :]
        rows = slice(first * own, (first + count) * own)
        query_x = jnp.concatenate([ref[...] for ref in query_refs], axis=0)
        query_y = mapped_ref[rows, :]
        sums = [total_ref[c, rows, :] for c in range(outs_n)]
        for k in range(0, len(blocks), 2):
            parts = query_sums(query_x, query_y, *center_terms(block_refs[k : k + 2], metric_ref[...], own, outs_n))
            sums = [a + b for a, b in zip(sums, parts)]
        for q in range(count):
            for c in range(outs_n):
                out_refs[q][c * own : (c + 1) * own, :] = sums[c][q * own : (q + 1) * own, :]

    args = list(queries) + list(blocks) + [metric, total, mapped]
    centers = sum(b.shape[0] for b in blocks)
    flops = 12 * centers * width * width + 12 * count * own * centers * width
    return call(body, tuple(shape(outs_n * own, width) for _ in queries), args, flops)


def upper_tiles(width):
    tile = 128 if width % 128 == 0 else width
    span = width // tile
    return tile, span, [(i, j) for i in range(span) for j in range(i, span)]


def outer_halves(part, arrived, metric):
    width = part.shape[1]
    tile, span, upper = upper_tiles(width)
    half = (len(upper) + 1) // 2

    def body(part_ref, arrived_ref, metric_ref, keep_ref, send_ref):
        odd = (lax.axis_index("col") & 1) == 1
        grads = dot(part_ref[...] + arrived_ref[...], metric_ref[...])
        tiles = [[] for _ in upper]
        for i in range(span):
            slab = dot(grads[:, i * tile : (i + 1) * tile], grads[:, i * tile :], (((0,), (0,)), ((), ())))
            for j in range(i, span):
                tiles[upper.index((i, j))] = slab[:, (j - i) * tile : (j - i + 1) * tile]
        while len(tiles) < 2 * half:
            tiles.append(jnp.zeros((tile, tile), jnp.float32))
        for k in range(half):
            keep_ref[k * tile : (k + 1) * tile, :] = jnp.where(odd, tiles[half + k], tiles[k])
            send_ref[k * tile : (k + 1) * tile, :] = jnp.where(odd, tiles[k], tiles[half + k])

    out = shape(half * tile, tile)
    return call(body, (out, out), [part, arrived, metric], 24 * part.shape[0] * width * width)


def finish(keep, other, points):
    rows, width = points.shape
    tile, span, upper = upper_tiles(width)
    half = (len(upper) + 1) // 2

    def body(keep_ref, other_ref, points_ref, next_ref, mapped_ref):
        odd = (lax.axis_index("col") & 1) == 1
        kept = [keep_ref[k * tile : (k + 1) * tile, :] for k in range(half)]
        came = [other_ref[k * tile : (k + 1) * tile, :] for k in range(half)]
        tiles = [jnp.where(odd, b, a) for a, b in zip(kept, came)]
        tiles += [jnp.where(odd, a, b) for a, b in zip(kept, came)]
        final = dict(zip(upper, tiles))
        diag = final[0, 0]
        for i in range(1, span):
            diag = diag + final[i, i]
        eye = lax.broadcasted_iota(jnp.int32, diag.shape, 0) == lax.broadcasted_iota(jnp.int32, diag.shape, 1)
        trace = jnp.sum(jnp.where(eye, diag, 0.0), keepdims=True)
        scale = width / trace
        for i, j in upper:
            value = final[i, j] * scale
            next_ref[i * tile : (i + 1) * tile, j * tile : (j + 1) * tile] = value
            if i != j:
                next_ref[j * tile : (j + 1) * tile, i * tile : (i + 1) * tile] = value.T
        mapped_ref[...] = dot(points_ref[...], next_ref[...])

    return call(body, (shape(width, width), shape(rows, width)), [keep, other, points], 12 * rows * width * width)


def make_local(rows_all, cols_all):
    hop = make_hop(rows_all, cols_all)
    row_bits = bits_of(rows_all)
    col_bits = bits_of(cols_all)
    bit_a, bit_b = row_bits[0], row_bits[1]
    line_bits = row_bits[2:]

    def to_a(value):
        return hop(value, (bit_a, 0), (bit_b, 0))

    def to_b(value):
        return hop(value, (bit_b, 0), (bit_a, 0))

    def over_cols(block):
        have = [block]
        for bit in col_bits:
            have = have + [hop(piece, (0, bit)) for piece in have]
        return have

    def local(points, coeffs, metric):
        own, width = points.shape
        outs_n = coeffs.shape[1]
        have = [pack_own(points, coeffs)]
        for bit in reversed(line_bits):
            have = have + [hop(piece, (bit, 0)) for piece in have]
        from_a = to_a(points)
        from_b = to_b(points)
        from_ab = to_b(from_a)
        early = over_cols(jnp.concatenate(have[:-1], axis=0))
        late = over_cols(have[-1])

        queries = [from_ab, from_a, from_b, points]
        total, mapped = early_sums(queries, early, metric, outs_n)
        part_ab, part_a = late_sums(queries[:2], 0, total, mapped, late, metric, outs_n)
        sent_ab, sent_a = to_a(part_ab), to_a(part_a)
        part_b, part_own = late_sums(queries[2:], 2, total, mapped, late, metric, outs_n)
        sent_b = to_b(part_b + sent_ab)

        keep, send = outer_halves(part_own + sent_a, sent_b, metric)
        keep = keep + hop(send, (0, 1))
        rest = [(bit, 0) for bit in row_bits]
        turn = len(rest) // 2
        for even_hop, odd_hop in zip(rest, rest[turn:] + rest[:turn]):
            keep = keep + hop(keep, even_hop, odd_hop)
        for bit in col_bits[1:]:
            keep = keep + hop(keep, (0, bit))
        return finish(keep, hop(keep, (0, 1)), points)

    return local


def solution(mesh):
    return jax.shard_map(
        make_local(mesh.shape["row"], mesh.shape["col"]),
        mesh=mesh,
        in_specs=(P(AXES, None), P(AXES, None), P()),
        out_specs=(P(), P(AXES, None)),
        check_vma=False,
    )
```

```python
import jax
import jax.numpy as jnp
from jax import lax
from jax.experimental import pallas as pl
from jax.experimental.pallas import tpu as pltpu
from jax.sharding import PartitionSpec as P

AXES = ("row", "col")
F32, BF16 = jnp.float32, jnp.bfloat16


def halves(x):
    high = x.astype(BF16)
    return high, (x - high.astype(F32)).astype(BF16)


def left(x, axis=1):
    high, low = halves(x)
    return jnp.concatenate([high, high, low], axis=axis)


def right(x, axis=1):
    high, low = halves(x)
    return jnp.concatenate([high, low, high], axis=axis)


def mul(a, b, da=1, db=0):
    return lax.dot_general(a, b, (((da,), (db,)), ((), ())), preferred_element_type=F32)


def round_up(count, step):
    return -(-count // step) * step


def bits_of(count):
    assert count & (count - 1) == 0
    return [1 << b for b in range(count.bit_length() - 1)]


def make_hop(rows, cols):
    def hop(value, even, odd=None):
        odd = even if odd is None else odd
        pairs = []
        for r in range(rows):
            for c in range(cols):
                dr, dc = odd if c & 1 else even
                pairs.append((r * cols + c, (r ^ dr) * cols + (c ^ dc)))
        return lax.ppermute(value, AXES, pairs)

    return hop


def call(body, out_shape, args, flops):
    moved = sum(4 * a.size for a in args) + sum(4 * s.size for s in jax.tree.leaves(out_shape))
    return pl.pallas_call(
        body,
        out_shape=out_shape,
        in_specs=[pl.BlockSpec(memory_space=pltpu.VMEM)] * len(args),
        out_specs=jax.tree.map(lambda _: pl.BlockSpec(memory_space=pltpu.VMEM), out_shape),
        compiler_params=pltpu.CompilerParams(vmem_limit_bytes=40 * 1024 * 1024),
        cost_estimate=pl.CostEstimate(flops=flops, bytes_accessed=moved, transcendentals=0),
    )(*args)


def shape(*dims):
    return jax.ShapeDtypeStruct(dims, F32)


def pack_own(points, coeffs):
    rows, width = points.shape
    outs_n = coeffs.shape[1]
    extra = round_up(outs_n + 1, 8)

    def body(points_ref, cols_ref, out_ref):
        out_ref[0:rows, :] = points_ref[...]
        out_ref[rows:, :] = jnp.zeros((extra, width), F32)
        cols = cols_ref[...]
        out_ref[rows : rows + outs_n, 0 : 2 * rows] = jnp.concatenate([cols, cols], axis=1)

    return call(body, shape(rows + extra, width), [points, coeffs.T], 1)


def norm_rows(centers, metric3, own):
    column = jnp.sum(centers * mul(left(centers), metric3), axis=1, keepdims=True)
    pair = 2 * own
    return [
        jnp.broadcast_to(column[k : k + pair], (pair, round_up(pair, 128))).T[0:1]
        for k in range(0, centers.shape[0], pair)
    ]


def join_blocks(packed, queries, metric, own, outs_n):
    height, width = packed[0].shape
    blocks, count = len(packed), len(queries)

    def body(*refs):
        packed_refs, query_refs = refs[:blocks], refs[blocks : blocks + count]
        metric_ref, joined_ref, mapped_ref, metric3_ref = refs[blocks + count :]
        metric3 = right(metric_ref[...], axis=0)
        metric3_ref[...] = metric3
        query_x = jnp.concatenate([ref[...] for ref in query_refs], axis=0)
        mapped_ref[...] = mul(left(query_x), metric3)
        doubled = []
        for k, ref in enumerate(packed_refs):
            joined_ref[k * height : (k + 1) * height, :] = ref[...]
            doubled += [ref[0:own, :], ref[0:own, :]]
        norms = norm_rows(jnp.concatenate(doubled, axis=0), metric3, own)
        for k, norm in enumerate(norms):
            row = k * height + own + outs_n
            joined_ref[row : row + 1, 0 : 2 * own] = norm

    out = (shape(blocks * height, width), shape(count * own, width), jax.ShapeDtypeStruct((3 * width, width), BF16))
    flops = 6 * (2 * blocks + count) * own * width * width
    return call(body, out, list(packed) + list(queries) + [metric], flops)


def center_terms(refs, own, outs_n, metric3=None):
    pieces, extras = [], []
    height = own + round_up(outs_n + 1, 8)
    for ref in refs:
        for first in range(0, ref.shape[0], height):
            pieces.append(ref[first : first + own, :])
            extras.append(ref[first + own : first + height, 0 : 2 * own])
    centers = jnp.concatenate(pieces, axis=0)
    lane = lax.broadcasted_iota(jnp.int32, extras[0].shape, 1)
    merged = [jnp.where(lane < own, extras[k], extras[k + 1]) for k in range(0, len(extras), 2)]
    rows = jnp.concatenate(merged, axis=1)
    if metric3 is None:
        norm = rows[outs_n : outs_n + 1]
    else:
        norm = jnp.concatenate(norm_rows(centers, metric3, own), axis=1)
    return centers, norm, [rows[c : c + 1] for c in range(outs_n)]


def query_sums(query_x, query_y, centers, norm, coefs):
    query_n = jnp.sum(query_x * query_y, axis=1, keepdims=True)
    cross = mul(left(query_y), right(centers), 1, 1)
    distance = jnp.sqrt(jnp.maximum(query_n + norm - 2.0 * cross, 0.0))
    weights = jnp.exp(-distance) / jnp.maximum(distance, 0.5)
    low = centers.astype(BF16)
    parts = []
    for coef in coefs:
        scaled = weights * coef
        sums = jnp.sum(scaled, axis=1, keepdims=True)
        parts.append(sums * query_x - mul(scaled.astype(BF16), low))
    return parts


def early_sums(queries, mapped, metric3, blocks, outs_n):
    own, width = queries[0].shape
    count = len(queries)

    def body(*refs):
        query_refs, block_refs = refs[:count], refs[count : count + len(blocks)]
        mapped_ref, metric3_ref, total_ref, first_ref = refs[count + len(blocks) :]
        query_x = jnp.concatenate([ref[...] for ref in query_refs], axis=0)
        first_y = mul(left(query_refs[0][...]), metric3_ref[...])
        first_ref[...] = first_y
        query_y = jnp.concatenate([first_y, mapped_ref[...]], axis=0)
        for k in range(0, len(blocks), 2):
            parts = query_sums(query_x, query_y, *center_terms(block_refs[k : k + 2], own, outs_n))
            for c in range(outs_n):
                if k == 0:
                    total_ref[c] = parts[c]
                else:
                    total_ref[c] = total_ref[c] + parts[c]

    args = list(queries) + list(blocks) + [mapped, metric3]
    centers = sum(b.shape[0] for b in blocks)
    flops = 6 * own * width * width + 10 * count * own * centers * width
    return call(body, (shape(outs_n, count * own, width), shape(own, width)), args, flops)


def late_sums(queries, mapped, spans, first, total, metric3, blocks, outs_n):
    own, width = queries[0].shape
    count, maps = len(queries), len(mapped)

    def body(*refs):
        query_refs, block_refs = refs[:count], refs[count : count + len(blocks)]
        mapped_refs = refs[count + len(blocks) : count + len(blocks) + maps]
        total_ref, metric3_ref = refs[count + len(blocks) + maps : count + len(blocks) + maps + 2]
        out_refs = refs[count + len(blocks) + maps + 2 :]
        rows = slice(first * own, (first + count) * own)
        query_x = jnp.concatenate([ref[...] for ref in query_refs], axis=0)
        query_y = [ref[a * own : b * own, :] for ref, (a, b) in zip(mapped_refs, spans)]
        query_y = query_y[0] if maps == 1 else jnp.concatenate(query_y, axis=0)
        sums = [total_ref[c, rows, :] for c in range(outs_n)]
        for k in range(0, len(blocks), 2):
            terms = center_terms(block_refs[k : k + 2], own, outs_n, metric3_ref[...])
            sums = [a + b for a, b in zip(sums, query_sums(query_x, query_y, *terms))]
        for q in range(count):
            for c in range(outs_n):
                out_refs[q][c * own : (c + 1) * own, :] = sums[c][q * own : (q + 1) * own, :]

    args = list(queries) + list(blocks) + list(mapped) + [total, metric3]
    centers = sum(b.shape[0] for b in blocks)
    flops = 6 * centers * width * width + 10 * count * own * centers * width
    return call(body, tuple(shape(outs_n * own, width) for _ in queries), args, flops)


def upper_tiles(width):
    tile = 128 if width % 128 == 0 else width
    span = width // tile
    return tile, span, [(i, j) for i in range(span) for j in range(i, span)]


def outer_halves(part, arrived, metric3):
    width = part.shape[1]
    tile, span, upper = upper_tiles(width)
    half = (len(upper) + 1) // 2

    def body(part_ref, arrived_ref, metric3_ref, keep_ref, send_ref):
        odd = (lax.axis_index("col") & 1) == 1
        grads = mul(left(part_ref[...] + arrived_ref[...]), metric3_ref[...])
        grads_left, grads_right = left(grads, 0), right(grads, 0)
        tiles = [[] for _ in upper]
        for i in range(span):
            slab = mul(grads_left[:, i * tile : (i + 1) * tile], grads_right[:, i * tile :], 0, 0)
            for j in range(i, span):
                tiles[upper.index((i, j))] = slab[:, (j - i) * tile : (j - i + 1) * tile]
        while len(tiles) < 2 * half:
            tiles.append(jnp.zeros((tile, tile), F32))
        for k in range(half):
            keep_ref[k * tile : (k + 1) * tile, :] = jnp.where(odd, tiles[half + k], tiles[k])
            send_ref[k * tile : (k + 1) * tile, :] = jnp.where(odd, tiles[k], tiles[half + k])

    out = shape(half * tile, tile)
    return call(body, (out, out), [part, arrived, metric3], 12 * part.shape[0] * width * width)


def finish(keep, other, points):
    rows, width = points.shape
    tile, span, upper = upper_tiles(width)
    half = (len(upper) + 1) // 2

    def body(keep_ref, other_ref, points_ref, next_ref, mapped_ref):
        odd = (lax.axis_index("col") & 1) == 1
        kept = [keep_ref[k * tile : (k + 1) * tile, :] for k in range(half)]
        came = [other_ref[k * tile : (k + 1) * tile, :] for k in range(half)]
        tiles = [jnp.where(odd, b, a) for a, b in zip(kept, came)]
        tiles += [jnp.where(odd, a, b) for a, b in zip(kept, came)]
        final = dict(zip(upper, tiles))
        diag = final[0, 0]
        for i in range(1, span):
            diag = diag + final[i, i]
        eye = lax.broadcasted_iota(jnp.int32, diag.shape, 0) == lax.broadcasted_iota(jnp.int32, diag.shape, 1)
        trace = jnp.sum(jnp.where(eye, diag, 0.0), keepdims=True)
        scale = width / trace
        for i, j in upper:
            value = final[i, j] * scale
            next_ref[i * tile : (i + 1) * tile, j * tile : (j + 1) * tile] = value
            if i != j:
                next_ref[j * tile : (j + 1) * tile, i * tile : (i + 1) * tile] = value.T
        mapped_ref[...] = mul(left(points_ref[...]), right(next_ref[...], axis=0))

    return call(body, (shape(width, width), shape(rows, width)), [keep, other, points], 6 * rows * width * width)


def make_local(rows_all, cols_all):
    hop = make_hop(rows_all, cols_all)
    row_bits = bits_of(rows_all)
    col_bits = bits_of(cols_all)
    bit_a, bit_b = row_bits[0], row_bits[1]
    line_bits = row_bits[2:]

    def to_a(value):
        return hop(value, (bit_a, 0), (bit_b, 0))

    def to_b(value):
        return hop(value, (bit_b, 0), (bit_a, 0))

    def over_cols(block):
        have = [block]
        for bit in col_bits:
            have = have + [hop(piece, (0, bit)) for piece in have]
        return have

    def local(points, coeffs, metric):
        own, width = points.shape
        outs_n = coeffs.shape[1]
        have = [pack_own(points, coeffs)]
        for bit in reversed(line_bits):
            have = have + [hop(piece, (bit, 0)) for piece in have]
        from_a = to_a(points)
        from_b = to_b(points)
        from_ab = to_b(from_a)
        queries = [from_ab, from_a, from_b, points]
        joined, mapped, metric3 = join_blocks(have[:-1], queries[1:], metric, own, outs_n)
        early, late = over_cols(joined), over_cols(have[-1])
        total, mapped_ab = early_sums(queries, mapped, metric3, early, outs_n)
        part_ab, part_a = late_sums(
            queries[:2], [mapped_ab, mapped], [(0, 1), (0, 1)], 0, total, metric3, late, outs_n
        )
        sent_ab, sent_a = to_a(part_ab), to_a(part_a)
        part_b, part_own = late_sums(queries[2:], [mapped], [(1, 3)], 2, total, metric3, late, outs_n)
        sent_b = to_b(part_b + sent_ab)

        keep, send = outer_halves(part_own + sent_a, sent_b, metric3)
        keep = keep + hop(send, (0, 1))
        rest = [(bit, 0) for bit in row_bits]
        turn = len(rest) // 2
        for even_hop, odd_hop in zip(rest, rest[turn:] + rest[:turn]):
            keep = keep + hop(keep, even_hop, odd_hop)
        for bit in col_bits[1:]:
            keep = keep + hop(keep, (0, bit))
        return finish(keep, hop(keep, (0, 1)), points)

    return local


def solution(mesh):
    return jax.shard_map(
        make_local(mesh.shape["row"], mesh.shape["col"]),
        mesh=mesh,
        in_specs=(P(AXES, None), P(AXES, None), P()),
        out_specs=(P(), P(AXES, None)),
        check_vma=False,
    )
```

```python
import jax
import jax.numpy as jnp
from jax import lax
from jax.experimental import pallas as pl
from jax.experimental.pallas import tpu as pltpu
from jax.sharding import PartitionSpec as P

AXES = ("row", "col")
F32, BF16 = jnp.float32, jnp.bfloat16


def halves(x):
    high = x.astype(BF16)
    return high, (x - high.astype(F32)).astype(BF16)


def left(x, axis=1):
    high, low = halves(x)
    return jnp.concatenate([high, high, low], axis=axis)


def right(x, axis=1):
    high, low = halves(x)
    return jnp.concatenate([high, low, high], axis=axis)


def mul(a, b, da=1, db=0):
    return lax.dot_general(a, b, (((da,), (db,)), ((), ())), preferred_element_type=F32)


def round_up(count, step):
    return -(-count // step) * step


def bits_of(count):
    assert count & (count - 1) == 0
    return [1 << b for b in range(count.bit_length() - 1)]


def make_hop(rows, cols):
    def hop(value, even, odd=None):
        odd = even if odd is None else odd
        pairs = []
        for r in range(rows):
            for c in range(cols):
                dr, dc = odd if c & 1 else even
                pairs.append((r * cols + c, (r ^ dr) * cols + (c ^ dc)))
        return lax.ppermute(value, AXES, pairs)

    return hop


def call(body, out_shape, args, flops):
    moved = sum(4 * a.size for a in args) + sum(4 * s.size for s in jax.tree.leaves(out_shape))
    return pl.pallas_call(
        body,
        out_shape=out_shape,
        in_specs=[pl.BlockSpec(memory_space=pltpu.VMEM)] * len(args),
        out_specs=jax.tree.map(lambda _: pl.BlockSpec(memory_space=pltpu.VMEM), out_shape),
        compiler_params=pltpu.CompilerParams(vmem_limit_bytes=40 * 1024 * 1024),
        cost_estimate=pl.CostEstimate(flops=flops, bytes_accessed=moved, transcendentals=0),
    )(*args)


def shape(*dims):
    return jax.ShapeDtypeStruct(dims, F32)


def pack_own(points, coeffs):
    rows, width = points.shape
    outs_n = coeffs.shape[1]
    extra = round_up(outs_n + 1, 8)

    def body(points_ref, cols_ref, plain_ref, packed_ref, cols_held, sems):
        copies = [
            pltpu.make_async_copy(points_ref, plain_ref, sems.at[0]),
            pltpu.make_async_copy(cols_ref, cols_held, sems.at[1]),
        ]
        for copy in copies:
            copy.start()
        packed_ref[rows:, :] = jnp.zeros((extra, width), F32)
        copies[1].wait()
        cols = cols_held[...]
        packed_ref[rows : rows + outs_n, 0 : 2 * rows] = jnp.concatenate([cols, cols], axis=1)
        copies[0].wait()
        packed_ref[0:rows, :] = plain_ref[...]

    return pl.pallas_call(
        body,
        out_shape=(shape(rows, width), shape(rows + extra, width)),
        in_specs=[pl.BlockSpec(memory_space=pl.ANY)] * 2,
        out_specs=(pl.BlockSpec(memory_space=pltpu.VMEM),) * 2,
        scratch_shapes=[pltpu.VMEM((outs_n, rows), F32), pltpu.SemaphoreType.DMA((2,))],
    )(points, coeffs.T)


def metric_halves(metric):
    width = metric.shape[0]

    def body(metric_ref, out_ref):
        out_ref[...] = right(metric_ref[...], axis=0)

    return call(body, jax.ShapeDtypeStruct((3 * width, width), BF16), [metric], 1)


def norm_rows(centers, metric3, own):
    column = jnp.sum(centers * mul(left(centers), metric3), axis=1, keepdims=True)
    pair = 2 * own
    return [
        jnp.broadcast_to(column[k : k + pair], (pair, round_up(pair, 128))).T[0:1]
        for k in range(0, centers.shape[0], pair)
    ]


def join_blocks(packed, queries, metric3, own, outs_n):
    height, width = packed[0].shape
    blocks, count = len(packed), len(queries)

    def body(*refs):
        packed_refs, query_refs = refs[:blocks], refs[blocks : blocks + count]
        metric3_ref, joined_ref, mapped_ref = refs[blocks + count :]
        metric3 = metric3_ref[...]
        query_x = jnp.concatenate([ref[...] for ref in query_refs], axis=0)
        mapped_ref[...] = mul(left(query_x), metric3)
        doubled = []
        for k, ref in enumerate(packed_refs):
            joined_ref[k * height : (k + 1) * height, :] = ref[...]
            doubled += [ref[0:own, :], ref[0:own, :]]
        norms = norm_rows(jnp.concatenate(doubled, axis=0), metric3, own)
        for k, norm in enumerate(norms):
            row = k * height + own + outs_n
            joined_ref[row : row + 1, 0 : 2 * own] = norm

    out = (shape(blocks * height, width), shape(count * own, width))
    flops = 6 * (2 * blocks + count) * own * width * width
    return call(body, out, list(packed) + list(queries) + [metric3], flops)


def center_terms(refs, own, outs_n, metric3=None):
    pieces, extras = [], []
    height = own + round_up(outs_n + 1, 8)
    for ref in refs:
        for first in range(0, ref.shape[0], height):
            pieces.append(ref[first : first + own, :])
            extras.append(ref[first + own : first + height, 0 : 2 * own])
    centers = jnp.concatenate(pieces, axis=0)
    lane = lax.broadcasted_iota(jnp.int32, extras[0].shape, 1)
    merged = [jnp.where(lane < own, extras[k], extras[k + 1]) for k in range(0, len(extras), 2)]
    rows = jnp.concatenate(merged, axis=1)
    if metric3 is None:
        norm = rows[outs_n : outs_n + 1]
    else:
        norm = jnp.concatenate(norm_rows(centers, metric3, own), axis=1)
    return centers, norm, [rows[c : c + 1] for c in range(outs_n)]


def query_sums(query_x, query_y, centers, norm, coefs):
    query_n = jnp.sum(query_x * query_y, axis=1, keepdims=True)
    cross = mul(left(query_y), right(centers), 1, 1)
    distance = jnp.sqrt(jnp.maximum(query_n + norm - 2.0 * cross, 0.0))
    weights = jnp.exp(-distance) / jnp.maximum(distance, 0.5)
    low = centers.astype(BF16)
    parts = []
    for coef in coefs:
        scaled = weights * coef
        sums = jnp.sum(scaled, axis=1, keepdims=True)
        parts.append(sums * query_x - mul(scaled.astype(BF16), low))
    return parts


def early_sums(queries, mapped, metric3, blocks, outs_n):
    own, width = queries[0].shape
    count = len(queries)

    def body(*refs):
        query_refs, block_refs = refs[:count], refs[count : count + len(blocks)]
        mapped_ref, metric3_ref, total_ref, first_ref = refs[count + len(blocks) :]
        query_x = jnp.concatenate([ref[...] for ref in query_refs], axis=0)
        first_y = mul(left(query_refs[0][...]), metric3_ref[...])
        first_ref[...] = first_y
        query_y = jnp.concatenate([first_y, mapped_ref[...]], axis=0)
        for k in range(0, len(blocks), 2):
            parts = query_sums(query_x, query_y, *center_terms(block_refs[k : k + 2], own, outs_n))
            for c in range(outs_n):
                if k == 0:
                    total_ref[c] = parts[c]
                else:
                    total_ref[c] = total_ref[c] + parts[c]

    args = list(queries) + list(blocks) + [mapped, metric3]
    centers = sum(b.shape[0] for b in blocks)
    flops = 6 * own * width * width + 10 * count * own * centers * width
    return call(body, (shape(outs_n, count * own, width), shape(own, width)), args, flops)


def late_sums(queries, mapped, spans, first, total, metric3, blocks, outs_n):
    own, width = queries[0].shape
    count, maps = len(queries), len(mapped)

    def body(*refs):
        query_refs, block_refs = refs[:count], refs[count : count + len(blocks)]
        mapped_refs = refs[count + len(blocks) : count + len(blocks) + maps]
        total_ref, metric3_ref = refs[count + len(blocks) + maps : count + len(blocks) + maps + 2]
        out_refs = refs[count + len(blocks) + maps + 2 :]
        rows = slice(first * own, (first + count) * own)
        query_x = jnp.concatenate([ref[...] for ref in query_refs], axis=0)
        query_y = [ref[a * own : b * own, :] for ref, (a, b) in zip(mapped_refs, spans)]
        query_y = query_y[0] if maps == 1 else jnp.concatenate(query_y, axis=0)
        sums = [total_ref[c, rows, :] for c in range(outs_n)]
        for k in range(0, len(blocks), 2):
            terms = center_terms(block_refs[k : k + 2], own, outs_n, metric3_ref[...])
            sums = [a + b for a, b in zip(sums, query_sums(query_x, query_y, *terms))]
        for q in range(count):
            for c in range(outs_n):
                out_refs[q][c * own : (c + 1) * own, :] = sums[c][q * own : (q + 1) * own, :]

    args = list(queries) + list(blocks) + list(mapped) + [total, metric3]
    centers = sum(b.shape[0] for b in blocks)
    flops = 6 * centers * width * width + 10 * count * own * centers * width
    return call(body, tuple(shape(outs_n * own, width) for _ in queries), args, flops)


def upper_tiles(width):
    tile = 128 if width % 128 == 0 else width
    span = width // tile
    return tile, span, [(i, j) for i in range(span) for j in range(i, span)]


def outer_halves(part, arrived, metric3):
    width = part.shape[1]
    tile, span, upper = upper_tiles(width)
    half = (len(upper) + 1) // 2

    def body(part_ref, arrived_ref, metric3_ref, keep_ref, send_ref):
        odd = (lax.axis_index("col") & 1) == 1
        grads = mul(left(part_ref[...] + arrived_ref[...]), metric3_ref[...])
        grads_left, grads_right = left(grads, 0), right(grads, 0)
        tiles = [[] for _ in upper]
        for i in range(span):
            slab = mul(grads_left[:, i * tile : (i + 1) * tile], grads_right[:, i * tile :], 0, 0)
            for j in range(i, span):
                tiles[upper.index((i, j))] = slab[:, (j - i) * tile : (j - i + 1) * tile]
        while len(tiles) < 2 * half:
            tiles.append(jnp.zeros((tile, tile), F32))
        for k in range(half):
            keep_ref[k * tile : (k + 1) * tile, :] = jnp.where(odd, tiles[half + k], tiles[k])
            send_ref[k * tile : (k + 1) * tile, :] = jnp.where(odd, tiles[k], tiles[half + k])

    out = shape(half * tile, tile)
    return call(body, (out, out), [part, arrived, metric3], 12 * part.shape[0] * width * width)


def plane_place(k):
    row, odd = lax.axis_index("row") & 3, lax.axis_index("col") & 1
    if k in (1, 2):
        return row ^ jnp.where(odd == 1, 3 - k, k)
    return row ^ k


def quarter(ref, k):
    rows = ref.shape[0] // 4
    return pl.ds(pl.multiple_of(plane_place(k) * rows, rows), rows)


def split_quarters(kept, arrived):
    rows, width = kept.shape

    def body(kept_ref, arrived_ref, *out_refs):
        for k in range(4):
            place = quarter(kept_ref, k)
            out_refs[k][...] = kept_ref[place, :] + arrived_ref[place, :]

    return call(body, (shape(rows // 4, width),) * 4, [kept, arrived], 1)


def join_quarters(parts):
    rows, width = parts[0].shape

    def body(*refs):
        out_ref = refs[-1]
        for k in range(4):
            out_ref[quarter(out_ref, k), :] = refs[k][...]

    return call(body, shape(4 * rows, width), parts, 1)


def add_all(parts):
    def body(*refs):
        values = [ref[...] for ref in refs[:-1]]
        while len(values) > 1:
            values = [a + b for a, b in zip(values[::2], values[1::2])]
        refs[-1][...] = values[0]

    return call(body, shape(*parts[0].shape), parts, 1)


def finish(keep, other, points):
    rows, width = points.shape
    tile, span, upper = upper_tiles(width)
    half = (len(upper) + 1) // 2

    def body(keep_ref, other_ref, points_ref, next_ref, mapped_ref):
        odd = (lax.axis_index("col") & 1) == 1
        kept = [keep_ref[k * tile : (k + 1) * tile, :] for k in range(half)]
        came = [other_ref[k * tile : (k + 1) * tile, :] for k in range(half)]
        tiles = [jnp.where(odd, b, a) for a, b in zip(kept, came)]
        tiles += [jnp.where(odd, a, b) for a, b in zip(kept, came)]
        final = dict(zip(upper, tiles))
        diag = final[0, 0]
        for i in range(1, span):
            diag = diag + final[i, i]
        eye = lax.broadcasted_iota(jnp.int32, diag.shape, 0) == lax.broadcasted_iota(jnp.int32, diag.shape, 1)
        trace = jnp.sum(jnp.where(eye, diag, 0.0), keepdims=True)
        scale = width / trace
        for i, j in upper:
            value = final[i, j] * scale
            next_ref[i * tile : (i + 1) * tile, j * tile : (j + 1) * tile] = value
            if i != j:
                next_ref[j * tile : (j + 1) * tile, i * tile : (i + 1) * tile] = value.T
        mapped_ref[...] = mul(left(points_ref[...]), right(next_ref[...], axis=0))

    return call(body, (shape(width, width), shape(rows, width)), [keep, other, points], 6 * rows * width * width)


def make_local(rows_all, cols_all):
    hop = make_hop(rows_all, cols_all)
    row_bits = bits_of(rows_all)
    col_bits = bits_of(cols_all)
    bit_a, bit_b = row_bits[0], row_bits[1]
    line_bits = row_bits[2:]

    def to_a(value):
        return hop(value, (bit_a, 0), (bit_b, 0))

    def to_b(value):
        return hop(value, (bit_b, 0), (bit_a, 0))

    def in_plane(parts):
        return [to_a(parts[0]), to_b(parts[1]), hop(parts[2], (bit_a | bit_b, 0))]

    def among(value, shifts):
        steps = [(0, 0)]
        for dr, dc in shifts:
            steps = steps + [(r | dr, c | dc) for r, c in steps]
        return [value] + [hop(value, step) for step in steps[1:]]

    def over_cols(block):
        have = [block]
        for bit in col_bits:
            have = have + [hop(piece, (0, bit)) for piece in have]
        return have

    def local(points, coeffs, metric):
        own, width = points.shape
        outs_n = coeffs.shape[1]
        points, packed = pack_own(points, coeffs)
        metric3 = metric_halves(metric)
        have = [packed]
        for bit in reversed(line_bits):
            have = have + [hop(piece, (bit, 0)) for piece in have]
        from_a = to_a(points)
        from_b = to_b(points)
        from_ab = to_b(from_a)
        queries = [from_ab, from_a, from_b, points]
        joined, mapped = join_blocks(have[:-1], queries[1:], metric3, own, outs_n)
        early, late = over_cols(joined), over_cols(have[-1])
        total, mapped_ab = early_sums(queries, mapped, metric3, early, outs_n)
        part_ab, part_a = late_sums(
            queries[:2], [mapped_ab, mapped], [(0, 1), (0, 1)], 0, total, metric3, late, outs_n
        )
        sent_ab, sent_a = to_a(part_ab), to_a(part_a)
        part_b, part_own = late_sums(queries[2:], [mapped], [(1, 3)], 2, total, metric3, late, outs_n)
        sent_b = to_b(part_b + sent_ab)

        keep, send = outer_halves(part_own + sent_a, sent_b, metric3)
        parts = split_quarters(keep, hop(send, (0, 1)))
        total = add_all([parts[0]] + in_plane(parts[1:]))
        for k in range(0, len(line_bits), 2):
            total = add_all(among(total, [(bit, 0) for bit in line_bits[k : k + 2]]))
        for bit in col_bits[1:]:
            total = add_all(among(total, [(0, bit)]))
        keep = join_quarters([total] + in_plane([total] * 3))
        return finish(keep, hop(keep, (0, 1)), points)

    return local


def solution(mesh):
    return jax.shard_map(
        make_local(mesh.shape["row"], mesh.shape["col"]),
        mesh=mesh,
        in_specs=(P(AXES, None), P(AXES, None), P()),
        out_specs=(P(), P(AXES, None)),
        check_vma=False,
    )
```

```python
import jax
import jax.numpy as jnp
from jax import lax
from jax.experimental import pallas as pl
from jax.experimental.pallas import tpu as pltpu
from jax.sharding import PartitionSpec as P

AXES = ("row", "col")
F32, BF16 = jnp.float32, jnp.bfloat16


def halves(x):
    high = x.astype(BF16)
    return high, (x - high.astype(F32)).astype(BF16)


def left(x, axis=1):
    high, low = halves(x)
    return jnp.concatenate([high, high, low], axis=axis)


def right(x, axis=1):
    high, low = halves(x)
    return jnp.concatenate([high, low, high], axis=axis)


def mul(a, b, da=1, db=0):
    return lax.dot_general(a, b, (((da,), (db,)), ((), ())), preferred_element_type=F32)


def round_up(count, step):
    return -(-count // step) * step


def bits_of(count):
    assert count & (count - 1) == 0
    return [1 << b for b in range(count.bit_length() - 1)]


def parity(x):
    return bin(x).count("1") & 1


def make_hop(rows, cols):
    def hop(value, even, odd=None):
        odd = even if odd is None else odd
        pairs = []
        for r in range(rows):
            for c in range(cols):
                dr, dc = odd if parity(r) ^ (c & 1) else even
                pairs.append((r * cols + c, (r ^ dr) * cols + (c ^ dc ^ parity(dr))))
        return lax.ppermute(value, AXES, pairs)

    return hop


def my_kind(rows):
    row, kind = lax.axis_index("row"), lax.axis_index("col")
    for bit in range(len(bits_of(rows))):
        kind = kind ^ (row >> bit)
    return kind & 1


def call(body, out_shape, args, flops):
    moved = sum(4 * a.size for a in args) + sum(4 * s.size for s in jax.tree.leaves(out_shape))
    return pl.pallas_call(
        body,
        out_shape=out_shape,
        in_specs=[pl.BlockSpec(memory_space=pltpu.VMEM)] * len(args),
        out_specs=jax.tree.map(lambda _: pl.BlockSpec(memory_space=pltpu.VMEM), out_shape),
        compiler_params=pltpu.CompilerParams(vmem_limit_bytes=40 * 1024 * 1024),
        cost_estimate=pl.CostEstimate(flops=flops, bytes_accessed=moved, transcendentals=0),
    )(*args)


def shape(*dims):
    return jax.ShapeDtypeStruct(dims, F32)


def pack_own(points, coeffs):
    rows, width = points.shape
    outs_n = coeffs.shape[1]
    extra = round_up(outs_n + 1, 8)

    def body(points_ref, cols_ref, plain_ref, packed_ref, cols_held, sems):
        copies = [
            pltpu.make_async_copy(points_ref, plain_ref, sems.at[0]),
            pltpu.make_async_copy(cols_ref, cols_held, sems.at[1]),
        ]
        for copy in copies:
            copy.start()
        packed_ref[rows:, :] = jnp.zeros((extra, width), F32)
        copies[1].wait()
        cols = cols_held[...]
        packed_ref[rows : rows + outs_n, 0 : 2 * rows] = jnp.concatenate([cols, cols], axis=1)
        copies[0].wait()
        packed_ref[0:rows, :] = plain_ref[...]

    return pl.pallas_call(
        body,
        out_shape=(pltpu.VMEM((rows, width), F32), pltpu.VMEM((rows + extra, width), F32)),
        in_specs=[pl.BlockSpec(memory_space=pl.ANY)] * 2,
        out_specs=(pl.BlockSpec(memory_space=pltpu.VMEM),) * 2,
        scratch_shapes=[pltpu.VMEM((outs_n, rows), F32), pltpu.SemaphoreType.DMA((2,))],
    )(points, coeffs.T)


def metric_halves(metric):
    width = metric.shape[0]

    def body(metric_ref, out_ref):
        out_ref[...] = right(metric_ref[...], axis=0)

    return call(body, jax.ShapeDtypeStruct((3 * width, width), BF16), [metric], 1)


def norm_rows(centers, metric3, own):
    column = jnp.sum(centers * mul(left(centers), metric3), axis=1, keepdims=True)
    pair = 2 * own
    rows = [
        jnp.broadcast_to(column[k : k + pair], (pair, round_up(pair, 128))).T[0:1]
        for k in range(0, centers.shape[0], pair)
    ]
    return jnp.concatenate(rows, axis=1)


def center_terms(refs, own, outs_n, metric3):
    pieces, extras = [], []
    height = own + round_up(outs_n + 1, 8)
    for ref in refs:
        for first in range(0, ref.shape[0], height):
            pieces.append(ref[first : first + own, :])
            extras.append(ref[first + own : first + height, 0 : 2 * own])
    centers = jnp.concatenate(pieces, axis=0)
    lane = lax.broadcasted_iota(jnp.int32, extras[0].shape, 1)
    merged = [jnp.where(lane < own, extras[k], extras[k + 1]) for k in range(0, len(extras), 2)]
    rows = jnp.concatenate(merged, axis=1)
    return centers, norm_rows(centers, metric3, own), [rows[c : c + 1] for c in range(outs_n)]


def query_sums(query_x, query_y, centers, norm, coefs):
    query_n = jnp.sum(query_x * query_y, axis=1, keepdims=True)
    cross = mul(left(query_y), right(centers), 1, 1)
    distance = jnp.sqrt(jnp.maximum(query_n + norm - 2.0 * cross, 0.0))
    weights = jnp.exp(-distance) / jnp.maximum(distance, 0.5)
    low = centers.astype(BF16)
    parts = []
    for coef in coefs:
        scaled = weights * coef
        sums = jnp.sum(scaled, axis=1, keepdims=True)
        parts.append(sums * query_x - mul(scaled.astype(BF16), low))
    return parts


def chunks(refs):
    return [refs[k : k + 8] for k in range(0, len(refs), 8)]


def early_sums(queries, blocks, metric3, outs_n):
    own, width = queries[0].shape
    count = len(queries)

    def body(*refs):
        query_refs, block_refs = refs[:count], refs[count : count + len(blocks)]
        metric3_ref, total_ref, mapped_ref = refs[count + len(blocks) :]
        query_x = jnp.concatenate([ref[...] for ref in query_refs], axis=0)
        query_y = mul(left(query_x), metric3_ref[...])
        mapped_ref[...] = query_y
        for k, run in enumerate(chunks(block_refs)):
            parts = query_sums(query_x, query_y, *center_terms(run, own, outs_n, metric3_ref[...]))
            for c in range(outs_n):
                total_ref[c] = parts[c] if k == 0 else total_ref[c] + parts[c]

    args = list(queries) + list(blocks) + [metric3]
    centers = sum(b.shape[0] for b in blocks)
    flops = 6 * (count * own + centers) * width * width + 10 * count * own * centers * width
    return call(body, (shape(outs_n, count * own, width), shape(count * own, width)), args, flops)


def late_sums(queries, first, total, mapped, metric3, blocks, outs_n):
    own, width = queries[0].shape
    count = len(queries)

    def body(*refs):
        query_refs, block_refs = refs[:count], refs[count : count + len(blocks)]
        total_ref, mapped_ref, metric3_ref = refs[count + len(blocks) : count + len(blocks) + 3]
        out_refs = refs[count + len(blocks) + 3 :]
        rows = slice(first * own, (first + count) * own)
        query_x = jnp.concatenate([ref[...] for ref in query_refs], axis=0)
        query_y = mapped_ref[rows, :]
        sums = [total_ref[c, rows, :] for c in range(outs_n)]
        for run in chunks(block_refs):
            terms = center_terms(run, own, outs_n, metric3_ref[...])
            sums = [a + b for a, b in zip(sums, query_sums(query_x, query_y, *terms))]
        for q in range(count):
            for c in range(outs_n):
                out_refs[q][c * own : (c + 1) * own, :] = sums[c][q * own : (q + 1) * own, :]

    args = list(queries) + list(blocks) + [total, mapped, metric3]
    centers = sum(b.shape[0] for b in blocks)
    flops = 6 * centers * width * width + 10 * count * own * centers * width
    return call(body, tuple(shape(outs_n * own, width) for _ in queries), args, flops)


def upper_tiles(width):
    tile = 128 if width % 128 == 0 else width
    span = width // tile
    return tile, span, [(i, j) for i in range(span) for j in range(i, span)]


def outer_halves(part, arrived, metric3, rows_all):
    width = part.shape[1]
    tile, span, upper = upper_tiles(width)
    half = (len(upper) + 1) // 2

    def body(part_ref, arrived_ref, metric3_ref, keep_ref, send_ref):
        odd = my_kind(rows_all) == 1
        grads = mul(left(part_ref[...] + arrived_ref[...]), metric3_ref[...])
        grads_left, grads_right = left(grads, 0), right(grads, 0)
        tiles = [[] for _ in upper]
        for i in range(span):
            slab = mul(grads_left[:, i * tile : (i + 1) * tile], grads_right[:, i * tile :], 0, 0)
            for j in range(i, span):
                tiles[upper.index((i, j))] = slab[:, (j - i) * tile : (j - i + 1) * tile]
        while len(tiles) < 2 * half:
            tiles.append(jnp.zeros((tile, tile), F32))
        for k in range(half):
            keep_ref[k * tile : (k + 1) * tile, :] = jnp.where(odd, tiles[half + k], tiles[k])
            send_ref[k * tile : (k + 1) * tile, :] = jnp.where(odd, tiles[k], tiles[half + k])

    out = shape(half * tile, tile)
    return call(body, (out, out), [part, arrived, metric3], 12 * part.shape[0] * width * width)


def plane_place(k, rows_all):
    row = lax.axis_index("row") & 3
    if k in (1, 2):
        return row ^ jnp.where(my_kind(rows_all) == 1, 3 - k, k)
    return row ^ k


def quarter(ref, k, rows_all):
    rows = ref.shape[0] // 4
    return pl.ds(pl.multiple_of(plane_place(k, rows_all) * rows, rows), rows)


def split_quarters(kept, arrived, rows_all):
    rows, width = kept.shape

    def body(kept_ref, arrived_ref, *out_refs):
        for k in range(4):
            place = quarter(kept_ref, k, rows_all)
            out_refs[k][...] = kept_ref[place, :] + arrived_ref[place, :]

    return call(body, (shape(rows // 4, width),) * 4, [kept, arrived], 1)


def join_quarters(parts, rows_all):
    rows, width = parts[0].shape

    def body(*refs):
        out_ref = refs[-1]
        for k in range(4):
            out_ref[quarter(out_ref, k, rows_all), :] = refs[k][...]

    return call(body, shape(4 * rows, width), parts, 1)


def add_all(parts):
    def body(*refs):
        values = [ref[...] for ref in refs[:-1]]
        while len(values) > 1:
            values = [a + b for a, b in zip(values[::2], values[1::2])]
        refs[-1][...] = values[0]

    return call(body, shape(*parts[0].shape), parts, 1)


def finish(keep, other, points, rows_all):
    rows, width = points.shape
    tile, span, upper = upper_tiles(width)
    half = (len(upper) + 1) // 2

    def body(keep_ref, other_ref, points_ref, next_ref, mapped_ref, next_held, mapped_held, sems):
        odd = my_kind(rows_all) == 1
        kept = [keep_ref[k * tile : (k + 1) * tile, :] for k in range(half)]
        came = [other_ref[k * tile : (k + 1) * tile, :] for k in range(half)]
        tiles = [jnp.where(odd, b, a) for a, b in zip(kept, came)]
        tiles += [jnp.where(odd, a, b) for a, b in zip(kept, came)]
        final = dict(zip(upper, tiles))
        diag = final[0, 0]
        for i in range(1, span):
            diag = diag + final[i, i]
        eye = lax.broadcasted_iota(jnp.int32, diag.shape, 0) == lax.broadcasted_iota(jnp.int32, diag.shape, 1)
        trace = jnp.sum(jnp.where(eye, diag, 0.0), keepdims=True)
        scale = width / trace
        for i, j in upper:
            value = final[i, j] * scale
            next_held[i * tile : (i + 1) * tile, j * tile : (j + 1) * tile] = value
            if i != j:
                next_held[j * tile : (j + 1) * tile, i * tile : (i + 1) * tile] = value.T
        next_copy = pltpu.make_async_copy(next_held, next_ref, sems.at[0])
        next_copy.start()
        mapped_held[...] = mul(left(points_ref[...]), right(next_held[...], axis=0))
        mapped_copy = pltpu.make_async_copy(mapped_held, mapped_ref, sems.at[1])
        mapped_copy.start()
        next_copy.wait()
        mapped_copy.wait()

    return pl.pallas_call(
        body,
        out_shape=(shape(width, width), shape(rows, width)),
        in_specs=[pl.BlockSpec(memory_space=pltpu.VMEM)] * 3,
        out_specs=(pl.BlockSpec(memory_space=pl.ANY),) * 2,
        scratch_shapes=[
            pltpu.VMEM((width, width), F32),
            pltpu.VMEM((rows, width), F32),
            pltpu.SemaphoreType.DMA((2,)),
        ],
        compiler_params=pltpu.CompilerParams(vmem_limit_bytes=40 * 1024 * 1024),
    )(keep, other, points)


def make_local(rows_all, cols_all):
    hop = make_hop(rows_all, cols_all)
    row_bits = bits_of(rows_all)
    col_bits = bits_of(cols_all)
    bit_a, bit_b = row_bits[0], row_bits[1]
    line_bits = row_bits[2:]

    def to_a(value):
        return hop(value, (bit_a, 0), (bit_b, 0))

    def to_b(value):
        return hop(value, (bit_b, 0), (bit_a, 0))

    def in_plane(parts):
        return [to_a(parts[0]), to_b(parts[1]), hop(parts[2], (bit_a | bit_b, 0))]

    def among(value, shifts):
        steps = [(0, 0)]
        for dr, dc in shifts:
            steps = steps + [(r | dr, c | dc) for r, c in steps]
        return [value] + [hop(value, step) for step in steps[1:]]

    def local(points, coeffs, metric):
        own, width = points.shape
        outs_n = coeffs.shape[1]
        points, packed = pack_own(points, coeffs)
        metric3 = metric_halves(metric)
        near = among(packed, [(bit, 0) for bit in reversed(line_bits)])
        from_a = to_a(points)
        from_b = to_b(points)
        queries = [to_b(from_a), from_a, from_b, points]
        total, mapped = early_sums(queries, near, metric3, outs_n)
        late = [other for block in near for other in among(block, [(0, bit) for bit in col_bits])[1:]]
        part_ab, part_a = late_sums(queries[:2], 0, total, mapped, metric3, late, outs_n)
        sent_ab, sent_a = to_a(part_ab), to_a(part_a)
        part_b, part_own = late_sums(queries[2:], 2, total, mapped, metric3, late, outs_n)
        sent_b = to_b(part_b + sent_ab)

        keep, send = outer_halves(part_own + sent_a, sent_b, metric3, rows_all)
        parts = split_quarters(keep, hop(send, (0, 1)), rows_all)
        total = add_all([parts[0]] + in_plane(parts[1:]))
        for k in range(0, len(line_bits), 2):
            total = add_all(among(total, [(bit, 0) for bit in line_bits[k : k + 2]]))
        for bit in col_bits[1:]:
            total = add_all(among(total, [(0, bit)]))
        keep = join_quarters([total] + in_plane([total] * 3), rows_all)
        return finish(keep, hop(keep, (0, 1)), points, rows_all)

    return local


def solution(mesh):
    return jax.shard_map(
        make_local(mesh.shape["row"], mesh.shape["col"]),
        mesh=mesh,
        in_specs=(P(AXES, None), P(AXES, None), P()),
        out_specs=(P(), P(AXES, None)),
        check_vma=False,
    )
```

```python
import jax
import jax.numpy as jnp
from jax import lax
from jax.experimental import pallas as pl
from jax.experimental.pallas import tpu as pltpu
from jax.sharding import PartitionSpec as P

AXES = ("row", "col")
F32, BF16 = jnp.float32, jnp.bfloat16


def halves(x):
    high = x.astype(BF16)
    return high, (x - high.astype(F32)).astype(BF16)


def left(x, axis=1):
    high, low = halves(x)
    return jnp.concatenate([high, high, low], axis=axis)


def right(x, axis=1):
    high, low = halves(x)
    return jnp.concatenate([high, low, high], axis=axis)


def mul(a, b, da=1, db=0):
    return lax.dot_general(a, b, (((da,), (db,)), ((), ())), preferred_element_type=F32)


def round_up(count, step):
    return -(-count // step) * step


def bits_of(count):
    assert count & (count - 1) == 0
    return [1 << b for b in range(count.bit_length() - 1)]


def parity(x):
    return bin(x).count("1") & 1


def make_hop(rows, cols):
    def hop(value, even, odd=None):
        odd = even if odd is None else odd
        pairs = []
        for r in range(rows):
            for c in range(cols):
                dr, dc = odd if parity(r) ^ (c & 1) else even
                pairs.append((r * cols + c, (r ^ dr) * cols + (c ^ dc ^ parity(dr))))
        return lax.ppermute(value, AXES, pairs)

    return hop


def my_kind(rows):
    row, kind = lax.axis_index("row"), lax.axis_index("col")
    for bit in range(len(bits_of(rows))):
        kind = kind ^ (row >> bit)
    return kind & 1


def call(body, out_shape, args, flops):
    moved = sum(4 * a.size for a in args) + sum(4 * s.size for s in jax.tree.leaves(out_shape))
    return pl.pallas_call(
        body,
        out_shape=out_shape,
        in_specs=[pl.BlockSpec(memory_space=pltpu.VMEM)] * len(args),
        out_specs=jax.tree.map(lambda _: pl.BlockSpec(memory_space=pltpu.VMEM), out_shape),
        compiler_params=pltpu.CompilerParams(vmem_limit_bytes=40 * 1024 * 1024),
        cost_estimate=pl.CostEstimate(flops=flops, bytes_accessed=moved, transcendentals=0),
    )(*args)


def shape(*dims):
    return jax.ShapeDtypeStruct(dims, F32)


def pack_own(points, coeffs):
    rows, width = points.shape
    outs_n = coeffs.shape[1]
    extra = round_up(outs_n + 1, 8)

    def body(points_ref, cols_ref, plain_ref, packed_ref, cols_held, sems):
        copies = [
            pltpu.make_async_copy(points_ref, plain_ref, sems.at[0]),
            pltpu.make_async_copy(cols_ref, cols_held, sems.at[1]),
        ]
        for copy in copies:
            copy.start()
        packed_ref[rows:, :] = jnp.zeros((extra, width), F32)
        copies[1].wait()
        cols = cols_held[...]
        packed_ref[rows : rows + outs_n, 0 : 2 * rows] = jnp.concatenate([cols, cols], axis=1)
        copies[0].wait()
        packed_ref[0:rows, :] = plain_ref[...]

    return pl.pallas_call(
        body,
        out_shape=(pltpu.VMEM((rows, width), F32), pltpu.VMEM((rows + extra, width), F32)),
        in_specs=[pl.BlockSpec(memory_space=pl.ANY)] * 2,
        out_specs=(pl.BlockSpec(memory_space=pltpu.VMEM),) * 2,
        scratch_shapes=[pltpu.VMEM((outs_n, rows), F32), pltpu.SemaphoreType.DMA((2,))],
    )(points, coeffs.T)


def copy_after(value, wanted):
    def body(value_ref, wanted_ref, out_ref):
        out_ref[...] = value_ref[...]

    return call(body, shape(*value.shape), [value, wanted], 1)


def metric_halves(metric):
    high = lax.reduce_precision(metric, 8, 7)
    low = (metric - high).astype(BF16)
    return jnp.concatenate([high.astype(BF16), low, high.astype(BF16)], axis=0)


def norm_rows(centers, metric3, own):
    column = jnp.sum(centers * mul(left(centers), metric3), axis=1, keepdims=True)
    pair = 2 * own
    rows = [
        jnp.broadcast_to(column[k : k + pair], (pair, round_up(pair, 128))).T[0:1]
        for k in range(0, centers.shape[0], pair)
    ]
    return jnp.concatenate(rows, axis=1)


def center_terms(refs, own, outs_n, metric3):
    pieces, extras = [], []
    height = own + round_up(outs_n + 1, 8)
    for ref in refs:
        for first in range(0, ref.shape[0], height):
            pieces.append(ref[first : first + own, :])
            extras.append(ref[first + own : first + height, 0 : 2 * own])
    centers = jnp.concatenate(pieces, axis=0)
    lane = lax.broadcasted_iota(jnp.int32, extras[0].shape, 1)
    merged = [jnp.where(lane < own, extras[k], extras[k + 1]) for k in range(0, len(extras), 2)]
    rows = jnp.concatenate(merged, axis=1)
    return centers, norm_rows(centers, metric3, own), [rows[c : c + 1] for c in range(outs_n)]


def query_sums(query_x, query_y, centers, norm, coefs):
    query_n = jnp.sum(query_x * query_y, axis=1, keepdims=True)
    cross = mul(left(query_y), right(centers), 1, 1)
    distance = jnp.sqrt(jnp.maximum(query_n + norm - 2.0 * cross, 0.0))
    weights = jnp.exp(-distance) / jnp.maximum(distance, 0.5)
    low = centers.astype(BF16)
    parts = []
    for coef in coefs:
        scaled = weights * coef
        sums = jnp.sum(scaled, axis=1, keepdims=True)
        parts.append(sums * query_x - mul(scaled.astype(BF16), low))
    return parts


def chunks(refs):
    return [refs[k : k + 8] for k in range(0, len(refs), 8)]


def early_sums(queries, blocks, metric3, outs_n):
    own, width = queries[0].shape
    count = len(queries)

    def body(*refs):
        query_refs, block_refs = refs[:count], refs[count : count + len(blocks)]
        metric3_ref, total_ref, mapped_ref = refs[count + len(blocks) :]
        query_x = jnp.concatenate([ref[...] for ref in query_refs], axis=0)
        query_y = mul(left(query_x), metric3_ref[...])
        mapped_ref[...] = query_y
        for k, run in enumerate(chunks(block_refs)):
            parts = query_sums(query_x, query_y, *center_terms(run, own, outs_n, metric3_ref[...]))
            for c in range(outs_n):
                total_ref[c] = parts[c] if k == 0 else total_ref[c] + parts[c]

    args = list(queries) + list(blocks) + [metric3]
    centers = sum(b.shape[0] for b in blocks)
    flops = 6 * (count * own + centers) * width * width + 10 * count * own * centers * width
    return call(body, (shape(outs_n, count * own, width), shape(count * own, width)), args, flops)


def late_sums(queries, first, total, mapped, metric3, blocks, outs_n):
    own, width = queries[0].shape
    count = len(queries)

    def body(*refs):
        query_refs, block_refs = refs[:count], refs[count : count + len(blocks)]
        total_ref, mapped_ref, metric3_ref = refs[count + len(blocks) : count + len(blocks) + 3]
        out_refs = refs[count + len(blocks) + 3 :]
        rows = slice(first * own, (first + count) * own)
        query_x = jnp.concatenate([ref[...] for ref in query_refs], axis=0)
        query_y = mapped_ref[rows, :]
        sums = [total_ref[c, rows, :] for c in range(outs_n)]
        for run in chunks(block_refs):
            terms = center_terms(run, own, outs_n, metric3_ref[...])
            sums = [a + b for a, b in zip(sums, query_sums(query_x, query_y, *terms))]
        for q in range(count):
            for c in range(outs_n):
                out_refs[q][c * own : (c + 1) * own, :] = sums[c][q * own : (q + 1) * own, :]

    args = list(queries) + list(blocks) + [total, mapped, metric3]
    centers = sum(b.shape[0] for b in blocks)
    flops = 6 * centers * width * width + 10 * count * own * centers * width
    return call(body, tuple(shape(outs_n * own, width) for _ in queries), args, flops)


def upper_tiles(width):
    tile = 128 if width % 128 == 0 else width
    span = width // tile
    return tile, span, [(i, j) for i in range(span) for j in range(i, span)]


def outer_halves(part, arrived, metric3, rows_all):
    width = part.shape[1]
    tile, span, upper = upper_tiles(width)
    half = (len(upper) + 1) // 2

    def body(part_ref, arrived_ref, metric3_ref, keep_ref, send_ref):
        odd = my_kind(rows_all) == 1
        grads = mul(left(part_ref[...] + arrived_ref[...]), metric3_ref[...])
        grads_left, grads_right = left(grads, 0), right(grads, 0)
        tiles = [[] for _ in upper]
        for i in range(span):
            slab = mul(grads_left[:, i * tile : (i + 1) * tile], grads_right[:, i * tile :], 0, 0)
            for j in range(i, span):
                tiles[upper.index((i, j))] = slab[:, (j - i) * tile : (j - i + 1) * tile]
        while len(tiles) < 2 * half:
            tiles.append(jnp.zeros((tile, tile), F32))
        for k in range(half):
            keep_ref[k * tile : (k + 1) * tile, :] = jnp.where(odd, tiles[half + k], tiles[k])
            send_ref[k * tile : (k + 1) * tile, :] = jnp.where(odd, tiles[k], tiles[half + k])

    out = shape(half * tile, tile)
    return call(body, (out, out), [part, arrived, metric3], 12 * part.shape[0] * width * width)


def plane_place(k, rows_all):
    row = lax.axis_index("row") & 3
    if k in (1, 2):
        return row ^ jnp.where(my_kind(rows_all) == 1, 3 - k, k)
    return row ^ k


def quarter(ref, k, rows_all):
    rows = ref.shape[0] // 4
    return pl.ds(pl.multiple_of(plane_place(k, rows_all) * rows, rows), rows)


def split_quarters(kept, arrived, rows_all):
    rows, width = kept.shape

    def body(kept_ref, arrived_ref, *out_refs):
        for k in range(4):
            place = quarter(kept_ref, k, rows_all)
            out_refs[k][...] = kept_ref[place, :] + arrived_ref[place, :]

    return call(body, (shape(rows // 4, width),) * 4, [kept, arrived], 1)


def join_quarters(parts, rows_all):
    rows, width = parts[0].shape

    def body(*refs):
        out_ref = refs[-1]
        for k in range(4):
            out_ref[quarter(out_ref, k, rows_all), :] = refs[k][...]

    return call(body, shape(4 * rows, width), parts, 1)


def add_all(parts):
    def body(*refs):
        values = [ref[...] for ref in refs[:-1]]
        while len(values) > 1:
            values = [a + b for a, b in zip(values[::2], values[1::2])]
        refs[-1][...] = values[0]

    return call(body, shape(*parts[0].shape), parts, 1)


def finish(keep, other, points, rows_all):
    rows, width = points.shape
    tile, span, upper = upper_tiles(width)
    half = (len(upper) + 1) // 2

    def body(keep_ref, other_ref, points_ref, next_ref, mapped_ref, next_held, mapped_held, sems):
        odd = my_kind(rows_all) == 1
        kept = [keep_ref[k * tile : (k + 1) * tile, :] for k in range(half)]
        came = [other_ref[k * tile : (k + 1) * tile, :] for k in range(half)]
        tiles = [jnp.where(odd, b, a) for a, b in zip(kept, came)]
        tiles += [jnp.where(odd, a, b) for a, b in zip(kept, came)]
        final = dict(zip(upper, tiles))
        diag = final[0, 0]
        for i in range(1, span):
            diag = diag + final[i, i]
        eye = lax.broadcasted_iota(jnp.int32, diag.shape, 0) == lax.broadcasted_iota(jnp.int32, diag.shape, 1)
        trace = jnp.sum(jnp.where(eye, diag, 0.0), keepdims=True)
        scale = width / trace
        for i, j in upper:
            value = final[i, j] * scale
            next_held[i * tile : (i + 1) * tile, j * tile : (j + 1) * tile] = value
            if i != j:
                next_held[j * tile : (j + 1) * tile, i * tile : (i + 1) * tile] = value.T
        next_copy = pltpu.make_async_copy(next_held, next_ref, sems.at[0])
        next_copy.start()
        mapped_held[...] = mul(left(points_ref[...]), right(next_held[...], axis=0))
        mapped_copy = pltpu.make_async_copy(mapped_held, mapped_ref, sems.at[1])
        mapped_copy.start()
        next_copy.wait()
        mapped_copy.wait()

    return pl.pallas_call(
        body,
        out_shape=(shape(width, width), shape(rows, width)),
        in_specs=[pl.BlockSpec(memory_space=pltpu.VMEM)] * 3,
        out_specs=(pl.BlockSpec(memory_space=pl.ANY),) * 2,
        scratch_shapes=[
            pltpu.VMEM((width, width), F32),
            pltpu.VMEM((rows, width), F32),
            pltpu.SemaphoreType.DMA((2,)),
        ],
        compiler_params=pltpu.CompilerParams(vmem_limit_bytes=40 * 1024 * 1024),
    )(keep, other, points)


def make_local(rows_all, cols_all):
    hop = make_hop(rows_all, cols_all)
    row_bits = bits_of(rows_all)
    col_bits = bits_of(cols_all)
    bit_a, bit_b = row_bits[0], row_bits[1]
    line_bits = row_bits[2:]

    def to_a(value):
        return hop(value, (bit_a, 0), (bit_b, 0))

    def to_b(value):
        return hop(value, (bit_b, 0), (bit_a, 0))

    def in_plane(parts):
        return [to_a(parts[0]), to_b(parts[1]), hop(parts[2], (bit_a | bit_b, 0))]

    def among(value, shifts):
        steps = [(0, 0)]
        for dr, dc in shifts:
            steps = steps + [(r | dr, c | dc) for r, c in steps]
        return [value] + [hop(value, step) for step in steps[1:]]

    def local(points, coeffs, metric):
        own, width = points.shape
        outs_n = coeffs.shape[1]
        points, packed = pack_own(points, coeffs)
        metric3 = metric_halves(metric)
        near = among(packed, [(bit, 0) for bit in reversed(line_bits)])
        late = [other for block in near for other in among(block, [(0, bit) for bit in col_bits])[1:]]
        source = copy_after(points, late[0])
        queries = [hop(source, (bit_a | bit_b, 0)), to_a(source), to_b(source), points]
        total, mapped = early_sums(queries, near, metric3, outs_n)
        (part_ab,) = late_sums(queries[:1], 0, total, mapped, metric3, late, outs_n)
        sent_ab = to_a(part_ab)
        (part_a,) = late_sums(queries[1:2], 1, total, mapped, metric3, late, outs_n)
        sent_a = to_a(part_a)
        part_b, part_own = late_sums(queries[2:], 2, total, mapped, metric3, late, outs_n)
        sent_b = to_b(part_b + sent_ab)

        keep, send = outer_halves(part_own + sent_a, sent_b, metric3, rows_all)
        parts = split_quarters(keep, hop(send, (0, 1)), rows_all)
        total = add_all([parts[0]] + in_plane(parts[1:]))
        for k in range(0, len(line_bits), 2):
            total = add_all(among(total, [(bit, 0) for bit in line_bits[k : k + 2]]))
        for bit in col_bits[1:]:
            total = add_all(among(total, [(0, bit)]))
        keep = join_quarters([total] + in_plane([total] * 3), rows_all)
        return finish(keep, hop(keep, (0, 1)), points, rows_all)

    return local


def solution(mesh):
    return jax.shard_map(
        make_local(mesh.shape["row"], mesh.shape["col"]),
        mesh=mesh,
        in_specs=(P(AXES, None), P(AXES, None), P()),
        out_specs=(P(), P(AXES, None)),
        check_vma=False,
    )
```

```python
import jax
import jax.numpy as jnp
from jax import lax
from jax.experimental import pallas as pl
from jax.experimental.pallas import tpu as pltpu
from jax.sharding import PartitionSpec as P

AXES = ("row", "col")
F32, BF16 = jnp.float32, jnp.bfloat16


def halves(x):
    high = x.astype(BF16)
    return high, (x - high.astype(F32)).astype(BF16)


def left(x, axis=1):
    high, low = halves(x)
    return jnp.concatenate([high, high, low], axis=axis)


def right(x, axis=1):
    high, low = halves(x)
    return jnp.concatenate([high, low, high], axis=axis)


def mul(a, b, da=1, db=0):
    return lax.dot_general(a, b, (((da,), (db,)), ((), ())), preferred_element_type=F32)


def round_up(count, step):
    return -(-count // step) * step


def bits_of(count):
    assert count & (count - 1) == 0
    return [1 << b for b in range(count.bit_length() - 1)]


def parity(x):
    return bin(x).count("1") & 1


def make_hop(rows, cols):
    def hop(value, even, odd=None):
        odd = even if odd is None else odd
        pairs = []
        for r in range(rows):
            for c in range(cols):
                dr, dc = odd if parity(r) ^ (c & 1) else even
                pairs.append((r * cols + c, (r ^ dr) * cols + (c ^ dc ^ parity(dr))))
        return lax.ppermute(value, AXES, pairs)

    return hop


def my_kind(rows):
    row, kind = lax.axis_index("row"), lax.axis_index("col")
    for bit in range(len(bits_of(rows))):
        kind = kind ^ (row >> bit)
    return kind & 1


def call(body, out_shape, args, flops):
    moved = sum(4 * a.size for a in args) + sum(4 * s.size for s in jax.tree.leaves(out_shape))
    return pl.pallas_call(
        body,
        out_shape=out_shape,
        in_specs=[pl.BlockSpec(memory_space=pltpu.VMEM)] * len(args),
        out_specs=jax.tree.map(lambda _: pl.BlockSpec(memory_space=pltpu.VMEM), out_shape),
        compiler_params=pltpu.CompilerParams(vmem_limit_bytes=40 * 1024 * 1024),
        cost_estimate=pl.CostEstimate(flops=flops, bytes_accessed=moved, transcendentals=0),
    )(*args)


def shape(*dims):
    return jax.ShapeDtypeStruct(dims, F32)


def pack_own(points, coeffs):
    rows, width = points.shape
    outs_n = coeffs.shape[1]
    extra = round_up(outs_n + 1, 8)

    def body(points_ref, cols_ref, plain_ref, packed_ref, cols_held, sems):
        copies = [
            pltpu.make_async_copy(points_ref, plain_ref, sems.at[0]),
            pltpu.make_async_copy(cols_ref, cols_held, sems.at[1]),
        ]
        for copy in copies:
            copy.start()
        packed_ref[rows:, :] = jnp.zeros((extra, width), F32)
        copies[1].wait()
        cols = cols_held[...]
        packed_ref[rows : rows + outs_n, 0 : 2 * rows] = jnp.concatenate([cols, cols], axis=1)
        copies[0].wait()
        packed_ref[0:rows, :] = plain_ref[...]

    return pl.pallas_call(
        body,
        out_shape=(pltpu.VMEM((rows, width), F32), pltpu.VMEM((rows + extra, width), F32)),
        in_specs=[pl.BlockSpec(memory_space=pl.ANY)] * 2,
        out_specs=(pl.BlockSpec(memory_space=pltpu.VMEM),) * 2,
        scratch_shapes=[pltpu.VMEM((outs_n, rows), F32), pltpu.SemaphoreType.DMA((2,))],
    )(points, coeffs.T)


def copy_after(value, wanted):
    def body(value_ref, wanted_ref, out_ref):
        out_ref[...] = value_ref[...]

    return call(body, shape(*value.shape), [value, wanted], 1)


def metric_halves(metric):
    high = lax.reduce_precision(metric, 8, 7)
    low = (metric - high).astype(BF16)
    return jnp.concatenate([high.astype(BF16), low, high.astype(BF16)], axis=0)


def norm_rows(centers, metric3, own):
    column = jnp.sum(centers * mul(left(centers), metric3), axis=1, keepdims=True)
    pair = 2 * own
    rows = [
        jnp.broadcast_to(column[k : k + pair], (pair, round_up(pair, 128))).T[0:1]
        for k in range(0, centers.shape[0], pair)
    ]
    return jnp.concatenate(rows, axis=1)


def center_terms(refs, own, outs_n, metric3):
    pieces, extras = [], []
    height = own + round_up(outs_n + 1, 8)
    for ref in refs:
        for first in range(0, ref.shape[0], height):
            pieces.append(ref[first : first + own, :])
            extras.append(ref[first + own : first + height, 0 : 2 * own])
    centers = jnp.concatenate(pieces, axis=0)
    lane = lax.broadcasted_iota(jnp.int32, extras[0].shape, 1)
    merged = [jnp.where(lane < own, extras[k], extras[k + 1]) for k in range(0, len(extras), 2)]
    rows = jnp.concatenate(merged, axis=1)
    return centers, norm_rows(centers, metric3, own), [rows[c : c + 1] for c in range(outs_n)]


def query_sums(query_x, query_y, centers, norm, coefs):
    query_n = jnp.sum(query_x * query_y, axis=1, keepdims=True)
    cross = mul(left(query_y), right(centers), 1, 1)
    distance = jnp.sqrt(jnp.maximum(query_n + norm - 2.0 * cross, 0.0))
    weights = jnp.exp(-distance) / jnp.maximum(distance, 0.5)
    low = centers.astype(BF16)
    parts = []
    for coef in coefs:
        scaled = weights * coef
        sums = jnp.sum(scaled, axis=1, keepdims=True)
        parts.append(sums * query_x - mul(scaled.astype(BF16), low))
    return parts


def chunks(refs):
    return [refs[k : k + 8] for k in range(0, len(refs), 8)]


def early_sums(queries, blocks, metric3, outs_n):
    own, width = queries[0].shape
    count = len(queries)

    def body(*refs):
        query_refs, block_refs = refs[:count], refs[count : count + len(blocks)]
        metric3_ref, total_ref, mapped_ref = refs[count + len(blocks) :]
        query_x = jnp.concatenate([ref[...] for ref in query_refs], axis=0)
        query_y = mul(left(query_x), metric3_ref[...])
        mapped_ref[...] = query_y
        for k, run in enumerate(chunks(block_refs)):
            parts = query_sums(query_x, query_y, *center_terms(run, own, outs_n, metric3_ref[...]))
            for c in range(outs_n):
                total_ref[c] = parts[c] if k == 0 else total_ref[c] + parts[c]

    args = list(queries) + list(blocks) + [metric3]
    centers = sum(b.shape[0] for b in blocks)
    flops = 6 * (count * own + centers) * width * width + 10 * count * own * centers * width
    return call(body, (shape(outs_n, count * own, width), shape(count * own, width)), args, flops)


def late_sums(queries, first, total, mapped, metric3, blocks, outs_n):
    own, width = queries[0].shape
    count = len(queries)

    def body(*refs):
        query_refs, block_refs = refs[:count], refs[count : count + len(blocks)]
        total_ref, mapped_ref, metric3_ref = refs[count + len(blocks) : count + len(blocks) + 3]
        out_refs = refs[count + len(blocks) + 3 :]
        rows = slice(first * own, (first + count) * own)
        query_x = jnp.concatenate([ref[...] for ref in query_refs], axis=0)
        query_y = mapped_ref[rows, :]
        sums = [total_ref[c, rows, :] for c in range(outs_n)]
        for run in chunks(block_refs):
            terms = center_terms(run, own, outs_n, metric3_ref[...])
            sums = [a + b for a, b in zip(sums, query_sums(query_x, query_y, *terms))]
        for q in range(count):
            for c in range(outs_n):
                out_refs[q][c * own : (c + 1) * own, :] = sums[c][q * own : (q + 1) * own, :]

    args = list(queries) + list(blocks) + [total, mapped, metric3]
    centers = sum(b.shape[0] for b in blocks)
    flops = 6 * centers * width * width + 10 * count * own * centers * width
    return call(body, tuple(shape(outs_n * own, width) for _ in queries), args, flops)


def upper_tiles(width):
    tile = 128 if width % 128 == 0 else width
    span = width // tile
    return tile, span, [(i, j) for i in range(span) for j in range(i, span)]


def outer_quarters(sums, metric3, rows_all):
    width = metric3.shape[1]
    tile, span, upper = upper_tiles(width)
    count = round_up(len(upper), 2)
    rows = count * tile // 4

    def body(*refs):
        metric3_ref, mine_ref, away_ref, full_ref = refs[len(sums) :]
        pairs = [refs[k][...] + refs[k + 1][...] for k in range(0, len(sums), 2)]
        grads = mul(left(jnp.concatenate(pairs, axis=0)), metric3_ref[...])
        grads_left, grads_right = left(grads, 0), right(grads, 0)
        for i in range(span):
            slab = mul(grads_left[:, i * tile : (i + 1) * tile], grads_right[:, i * tile :], 0, 0)
            for j in range(i, span):
                row = upper.index((i, j)) * tile
                full_ref[row : row + tile, :] = slab[:, (j - i) * tile : (j - i + 1) * tile]
        if count > len(upper):
            full_ref[len(upper) * tile :, :] = jnp.zeros(((count - len(upper)) * tile, tile), F32)
        for k, out_ref in enumerate([mine_ref, away_ref]):
            out_ref[...] = full_ref[quarter(full_ref, k, rows_all), :]

    out = shape(rows, tile)
    return pl.pallas_call(
        body,
        out_shape=(out, out),
        in_specs=[pl.BlockSpec(memory_space=pltpu.VMEM)] * (len(sums) + 1),
        out_specs=(pl.BlockSpec(memory_space=pltpu.VMEM),) * 2,
        scratch_shapes=[pltpu.VMEM((count * tile, tile), F32)],
        compiler_params=pltpu.CompilerParams(vmem_limit_bytes=40 * 1024 * 1024),
    )(*sums, metric3)


def plane_place(k, rows_all):
    row = lax.axis_index("row") & 3
    if k in (1, 2):
        return row ^ jnp.where(my_kind(rows_all) == 1, 3 - k, k)
    return row ^ k


def quarter(ref, k, rows_all):
    rows = ref.shape[0] // 4
    return pl.ds(pl.multiple_of(plane_place(k, rows_all) * rows, rows), rows)


def split_halves(mine, arrived, rows_all):
    rows, width = mine.shape
    half = rows // 2

    def body(mine_ref, arrived_ref, keep_ref, send_ref):
        kind = my_kind(rows_all)
        for place, out_ref in ((kind, keep_ref), (1 - kind, send_ref)):
            here = pl.ds(pl.multiple_of(place * half, half), half)
            out_ref[...] = mine_ref[here, :] + arrived_ref[here, :]

    return call(body, (shape(half, width),) * 2, [mine, arrived], 1)


def join_quarters(parts, rows_all):
    rows, width = parts[0].shape

    def body(*refs):
        out_ref = refs[-1]
        for k in range(4):
            out_ref[quarter(out_ref, k, rows_all), :] = refs[k][...]

    return call(body, shape(4 * rows, width), parts, 1)


def add_all(parts):
    def body(*refs):
        values = [ref[...] for ref in refs[:-1]]
        while len(values) > 1:
            values = [a + b for a, b in zip(values[::2], values[1::2])]
        refs[-1][...] = values[0]

    return call(body, shape(*parts[0].shape), parts, 1)


def finish(keep, other, points, rows_all):
    rows, width = points.shape
    tile, span, upper = upper_tiles(width)

    def body(keep_ref, other_ref, points_ref, next_ref, mapped_ref, next_held, mapped_held, sems):
        odd = my_kind(rows_all) == 1
        piece = keep_ref.shape[0] // 4
        rows_of = []
        for k in range(4):
            kept, came = (ref[k * piece : (k + 1) * piece, :] for ref in (keep_ref, other_ref))
            rows_of += [jnp.where(odd, came, kept), jnp.where(odd, kept, came)]
        full = jnp.concatenate(rows_of, axis=0)
        tiles = [full[k * tile : (k + 1) * tile] for k in range(len(upper))]
        final = dict(zip(upper, tiles))
        diag = final[0, 0]
        for i in range(1, span):
            diag = diag + final[i, i]
        eye = lax.broadcasted_iota(jnp.int32, diag.shape, 0) == lax.broadcasted_iota(jnp.int32, diag.shape, 1)
        trace = jnp.sum(jnp.where(eye, diag, 0.0), keepdims=True)
        scale = width / trace
        for i, j in upper:
            value = final[i, j] * scale
            next_held[i * tile : (i + 1) * tile, j * tile : (j + 1) * tile] = value
            if i != j:
                next_held[j * tile : (j + 1) * tile, i * tile : (i + 1) * tile] = value.T
        next_copy = pltpu.make_async_copy(next_held, next_ref, sems.at[0])
        next_copy.start()
        mapped_held[...] = mul(left(points_ref[...]), right(next_held[...], axis=0))
        mapped_copy = pltpu.make_async_copy(mapped_held, mapped_ref, sems.at[1])
        mapped_copy.start()
        next_copy.wait()
        mapped_copy.wait()

    return pl.pallas_call(
        body,
        out_shape=(shape(width, width), shape(rows, width)),
        in_specs=[pl.BlockSpec(memory_space=pltpu.VMEM)] * 3,
        out_specs=(pl.BlockSpec(memory_space=pl.ANY),) * 2,
        scratch_shapes=[
            pltpu.VMEM((width, width), F32),
            pltpu.VMEM((rows, width), F32),
            pltpu.SemaphoreType.DMA((2,)),
        ],
        compiler_params=pltpu.CompilerParams(vmem_limit_bytes=40 * 1024 * 1024),
    )(keep, other, points)


def make_local(rows_all, cols_all):
    hop = make_hop(rows_all, cols_all)
    row_bits = bits_of(rows_all)
    col_bits = bits_of(cols_all)
    bit_a, bit_b = row_bits[0], row_bits[1]
    line_bits = row_bits[2:]

    def to_a(value):
        return hop(value, (bit_a, 0), (bit_b, 0))

    def to_b(value):
        return hop(value, (bit_b, 0), (bit_a, 0))

    def in_plane(parts):
        return [to_a(parts[0]), to_b(parts[1]), hop(parts[2], (bit_a | bit_b, 0))]

    def among(value, shifts):
        steps = [(0, 0)]
        for dr, dc in shifts:
            steps = steps + [(r | dr, c | dc) for r, c in steps]
        return [value] + [hop(value, step) for step in steps[1:]]

    def local(points, coeffs, metric):
        own, width = points.shape
        outs_n = coeffs.shape[1]
        points, packed = pack_own(points, coeffs)
        metric3 = metric_halves(metric)
        near = among(packed, [(bit, 0) for bit in reversed(line_bits)])
        late = [other for block in near for other in among(block, [(0, bit) for bit in col_bits])[1:]]
        source = copy_after(points, late[0])
        queries = [hop(source, (bit_a | bit_b, 0)), to_a(source), to_b(source), points]
        total, mapped = early_sums(queries, near, metric3, outs_n)
        (part_ab,) = late_sums(queries[:1], 0, total, mapped, metric3, late, outs_n)
        sent_ab = to_a(part_ab)
        (part_a,) = late_sums(queries[1:2], 1, total, mapped, metric3, late, outs_n)
        sent_a = to_a(part_a)
        part_b, part_own = late_sums(queries[2:], 2, total, mapped, metric3, late, outs_n)
        half_b = part_b + sent_ab
        rest_own = to_b(half_b)
        half_own = part_own + sent_a
        rest_b = to_b(half_own)

        mine, away = outer_quarters([half_own, rest_own, half_b, rest_b], metric3, rows_all)
        keep, send = split_halves(mine, to_a(away), rows_all)
        total = add_all([keep, hop(send, (0, 1))])
        for k in range(0, len(line_bits), 2):
            total = add_all(among(total, [(bit, 0) for bit in line_bits[k : k + 2]]))
        for bit in col_bits[1:]:
            total = add_all(among(total, [(0, bit)]))
        keep = join_quarters([total] + in_plane([total] * 3), rows_all)
        return finish(keep, hop(keep, (0, 1)), points, rows_all)

    return local


def solution(mesh):
    return jax.shard_map(
        make_local(mesh.shape["row"], mesh.shape["col"]),
        mesh=mesh,
        in_specs=(P(AXES, None), P(AXES, None), P()),
        out_specs=(P(), P(AXES, None)),
        check_vma=False,
    )
```

```python
import jax
import jax.numpy as jnp
from jax import lax
from jax.experimental import pallas as pl
from jax.experimental.pallas import tpu as pltpu
from jax.sharding import PartitionSpec as P

AXES = ("row", "col")
F32, BF16 = jnp.float32, jnp.bfloat16


def halves(x):
    high = x.astype(BF16)
    return high, (x - high.astype(F32)).astype(BF16)


def left(x, axis=1):
    high, low = halves(x)
    return jnp.concatenate([high, high, low], axis=axis)


def right(x, axis=1):
    high, low = halves(x)
    return jnp.concatenate([high, low, high], axis=axis)


def mul(a, b, da=1, db=0):
    return lax.dot_general(a, b, (((da,), (db,)), ((), ())), preferred_element_type=F32)


def round_up(count, step):
    return -(-count // step) * step


def bits_of(count):
    assert count & (count - 1) == 0
    return [1 << b for b in range(count.bit_length() - 1)]


def parity(x):
    return bin(x).count("1") & 1


def make_hop(rows, cols):
    def hop(value, even, odd=None):
        odd = even if odd is None else odd
        pairs = []
        for r in range(rows):
            for c in range(cols):
                dr, dc = odd if parity(r) ^ (c & 1) else even
                pairs.append((r * cols + c, (r ^ dr) * cols + (c ^ dc ^ parity(dr))))
        return lax.ppermute(value, AXES, pairs)

    return hop


def my_kind(rows):
    row, kind = lax.axis_index("row"), lax.axis_index("col")
    for bit in range(len(bits_of(rows))):
        kind = kind ^ (row >> bit)
    return kind & 1


def call(body, out_shape, args, flops):
    moved = sum(4 * a.size for a in args) + sum(4 * s.size for s in jax.tree.leaves(out_shape))
    return pl.pallas_call(
        body,
        out_shape=out_shape,
        in_specs=[pl.BlockSpec(memory_space=pltpu.VMEM)] * len(args),
        out_specs=jax.tree.map(lambda _: pl.BlockSpec(memory_space=pltpu.VMEM), out_shape),
        compiler_params=pltpu.CompilerParams(vmem_limit_bytes=40 * 1024 * 1024),
        cost_estimate=pl.CostEstimate(flops=flops, bytes_accessed=moved, transcendentals=0),
    )(*args)


def shape(*dims):
    return jax.ShapeDtypeStruct(dims, F32)


def pack_own(points, coeffs):
    rows, width = points.shape
    outs_n = coeffs.shape[1]
    extra = round_up(outs_n + 1, 8)

    def body(points_ref, cols_ref, plain_ref, packed_ref, cols_held, sems):
        copies = [
            pltpu.make_async_copy(points_ref, plain_ref, sems.at[0]),
            pltpu.make_async_copy(cols_ref, cols_held, sems.at[1]),
        ]
        for copy in copies:
            copy.start()
        packed_ref[rows:, :] = jnp.zeros((extra, width), F32)
        copies[1].wait()
        cols = cols_held[...]
        packed_ref[rows : rows + outs_n, 0 : 2 * rows] = jnp.concatenate([cols, cols], axis=1)
        copies[0].wait()
        packed_ref[0:rows, :] = plain_ref[...]

    return pl.pallas_call(
        body,
        out_shape=(pltpu.VMEM((rows, width), F32), pltpu.VMEM((rows + extra, width), F32)),
        in_specs=[pl.BlockSpec(memory_space=pl.ANY)] * 2,
        out_specs=(pl.BlockSpec(memory_space=pltpu.VMEM),) * 2,
        scratch_shapes=[pltpu.VMEM((outs_n, rows), F32), pltpu.SemaphoreType.DMA((2,))],
    )(points, coeffs.T)


def copy_after(value, wanted):
    def body(value_ref, wanted_ref, out_ref):
        out_ref[...] = value_ref[...]

    return call(body, shape(*value.shape), [value, wanted], 1)


def metric_halves(metric):
    high = lax.reduce_precision(metric, 8, 7)
    low = (metric - high).astype(BF16)
    return jnp.concatenate([high.astype(BF16), low, high.astype(BF16)], axis=0)


def norm_rows(centers, metric3, own):
    column = jnp.sum(centers * mul(left(centers), metric3), axis=1, keepdims=True)
    pair = 2 * own
    rows = [
        jnp.broadcast_to(column[k : k + pair], (pair, round_up(pair, 128))).T[0:1]
        for k in range(0, centers.shape[0], pair)
    ]
    return jnp.concatenate(rows, axis=1)


def center_terms(refs, own, outs_n, metric3):
    pieces, extras = [], []
    height = own + round_up(outs_n + 1, 8)
    for ref in refs:
        for first in range(0, ref.shape[0], height):
            pieces.append(ref[first : first + own, :])
            extras.append(ref[first + own : first + height, 0 : 2 * own])
    centers = jnp.concatenate(pieces, axis=0)
    lane = lax.broadcasted_iota(jnp.int32, extras[0].shape, 1)
    merged = [jnp.where(lane < own, extras[k], extras[k + 1]) for k in range(0, len(extras), 2)]
    rows = jnp.concatenate(merged, axis=1)
    return centers, norm_rows(centers, metric3, own), [rows[c : c + 1] for c in range(outs_n)]


def query_sums(query_x, query_y, centers, norm, coefs):
    query_n = jnp.sum(query_x * query_y, axis=1, keepdims=True)
    cross = mul(left(query_y), right(centers), 1, 1)
    distance = jnp.sqrt(jnp.maximum(query_n + norm - 2.0 * cross, 0.0))
    weights = jnp.exp(-distance) / jnp.maximum(distance, 0.5)
    low = centers.astype(BF16)
    parts = []
    for coef in coefs:
        scaled = weights * coef
        sums = jnp.sum(scaled, axis=1, keepdims=True)
        parts.append(sums * query_x - mul(scaled.astype(BF16), low))
    return parts


def chunks(refs):
    return [refs[k : k + 8] for k in range(0, len(refs), 8)]


def early_sums(queries, blocks, metric3, outs_n):
    own, width = queries[0].shape
    count = len(queries)

    def body(*refs):
        query_refs, block_refs = refs[:count], refs[count : count + len(blocks)]
        metric3_ref, total_ref, mapped_ref = refs[count + len(blocks) :]
        query_x = jnp.concatenate([ref[...] for ref in query_refs], axis=0)
        query_y = mul(left(query_x), metric3_ref[...])
        mapped_ref[...] = query_y
        for k, run in enumerate(chunks(block_refs)):
            parts = query_sums(query_x, query_y, *center_terms(run, own, outs_n, metric3_ref[...]))
            for c in range(outs_n):
                total_ref[c] = parts[c] if k == 0 else total_ref[c] + parts[c]

    args = list(queries) + list(blocks) + [metric3]
    centers = sum(b.shape[0] for b in blocks)
    flops = 6 * (count * own + centers) * width * width + 10 * count * own * centers * width
    return call(body, (shape(outs_n, count * own, width), shape(count * own, width)), args, flops)


def late_sums(queries, first, total, mapped, metric3, blocks, outs_n, wanted=()):
    own, width = queries[0].shape
    count = len(queries)

    def body(*refs):
        query_refs, block_refs = refs[:count], refs[count : count + len(blocks)]
        total_ref, mapped_ref, metric3_ref = refs[count + len(blocks) : count + len(blocks) + 3]
        out_refs = refs[count + len(blocks) + 3 + len(wanted) :]
        rows = slice(first * own, (first + count) * own)
        query_x = jnp.concatenate([ref[...] for ref in query_refs], axis=0)
        query_y = mapped_ref[rows, :]
        sums = [total_ref[c, rows, :] for c in range(outs_n)]
        for run in chunks(block_refs):
            terms = center_terms(run, own, outs_n, metric3_ref[...])
            sums = [a + b for a, b in zip(sums, query_sums(query_x, query_y, *terms))]
        for q in range(count):
            for c in range(outs_n):
                out_refs[q][c * own : (c + 1) * own, :] = sums[c][q * own : (q + 1) * own, :]

    args = list(queries) + list(blocks) + [total, mapped, metric3] + list(wanted)
    centers = sum(b.shape[0] for b in blocks)
    flops = 6 * centers * width * width + 10 * count * own * centers * width
    return call(body, tuple(shape(outs_n * own, width) for _ in queries), args, flops)


def whole_sums(queries, blocks, metric3, outs_n):
    own, width = queries[0].shape
    count = len(queries)

    def body(*refs):
        query_refs, block_refs = refs[:count], refs[count : count + len(blocks)]
        metric3_ref, out_refs = refs[count + len(blocks)], refs[count + len(blocks) + 1 :]
        query_x = jnp.concatenate([ref[...] for ref in query_refs], axis=0)
        query_y = mul(left(query_x), metric3_ref[...])
        sums = None
        for run in chunks(block_refs):
            parts = query_sums(query_x, query_y, *center_terms(run, own, outs_n, metric3_ref[...]))
            sums = parts if sums is None else [a + b for a, b in zip(sums, parts)]
        for q in range(count):
            for c in range(outs_n):
                out_refs[q][c * own : (c + 1) * own, :] = sums[c][q * own : (q + 1) * own, :]

    args = list(queries) + list(blocks) + [metric3]
    centers = sum(b.shape[0] for b in blocks)
    flops = 6 * (count * own + centers) * width * width + 10 * count * own * centers * width
    return call(body, tuple(shape(outs_n * own, width) for _ in queries), args, flops)


def upper_tiles(width):
    tile = 128 if width % 128 == 0 else width
    span = width // tile
    return tile, span, [(i, j) for i in range(span) for j in range(i, span)]


def outer_quarters(sums, metric3, rows_all):
    width = metric3.shape[1]
    tile, span, upper = upper_tiles(width)
    count = round_up(len(upper), 2)
    rows = count * tile // 4

    def body(*refs):
        metric3_ref, mine_ref, away_ref, full_ref = refs[len(sums) :]
        pairs = [refs[k][...] + refs[k + 1][...] for k in range(0, len(sums), 2)]
        grads = mul(left(jnp.concatenate(pairs, axis=0)), metric3_ref[...])
        grads_left, grads_right = left(grads, 0), right(grads, 0)
        for i in range(span):
            slab = mul(grads_left[:, i * tile : (i + 1) * tile], grads_right[:, i * tile :], 0, 0)
            for j in range(i, span):
                row = upper.index((i, j)) * tile
                full_ref[row : row + tile, :] = slab[:, (j - i) * tile : (j - i + 1) * tile]
        if count > len(upper):
            full_ref[len(upper) * tile :, :] = jnp.zeros(((count - len(upper)) * tile, tile), F32)
        for k, out_ref in enumerate([mine_ref, away_ref]):
            out_ref[...] = full_ref[quarter(full_ref, k, rows_all), :]

    out = shape(rows, tile)
    return pl.pallas_call(
        body,
        out_shape=(out, out),
        in_specs=[pl.BlockSpec(memory_space=pltpu.VMEM)] * (len(sums) + 1),
        out_specs=(pl.BlockSpec(memory_space=pltpu.VMEM),) * 2,
        scratch_shapes=[pltpu.VMEM((count * tile, tile), F32)],
        compiler_params=pltpu.CompilerParams(vmem_limit_bytes=40 * 1024 * 1024),
    )(*sums, metric3)


def plane_place(k, rows_all):
    row = lax.axis_index("row") & 3
    if k in (1, 2):
        return row ^ jnp.where(my_kind(rows_all) == 1, 3 - k, k)
    return row ^ k


def quarter(ref, k, rows_all):
    rows = ref.shape[0] // 4
    return pl.ds(pl.multiple_of(plane_place(k, rows_all) * rows, rows), rows)


def split_halves(mine, arrived, rows_all):
    rows, width = mine.shape
    half = rows // 2

    def body(mine_ref, arrived_ref, keep_ref, send_ref):
        kind = my_kind(rows_all)
        for place, out_ref in ((kind, keep_ref), (1 - kind, send_ref)):
            here = pl.ds(pl.multiple_of(place * half, half), half)
            out_ref[...] = mine_ref[here, :] + arrived_ref[here, :]

    return call(body, (shape(half, width),) * 2, [mine, arrived], 1)


def join_quarters(parts, rows_all):
    rows, width = parts[0].shape

    def body(*refs):
        out_ref = refs[-1]
        for k in range(4):
            out_ref[quarter(out_ref, k, rows_all), :] = refs[k][...]

    return call(body, shape(4 * rows, width), parts, 1)


def add_all(parts):
    def body(*refs):
        values = [ref[...] for ref in refs[:-1]]
        while len(values) > 1:
            values = [a + b for a, b in zip(values[::2], values[1::2])]
        refs[-1][...] = values[0]

    return call(body, shape(*parts[0].shape), parts, 1)


def finish(keep, other, points, rows_all):
    rows, width = points.shape
    tile, span, upper = upper_tiles(width)

    def body(keep_ref, other_ref, points_ref, next_ref, mapped_ref, next_held, mapped_held, sems):
        odd = my_kind(rows_all) == 1
        piece = keep_ref.shape[0] // 4
        rows_of = []
        for k in range(4):
            kept, came = (ref[k * piece : (k + 1) * piece, :] for ref in (keep_ref, other_ref))
            rows_of += [jnp.where(odd, came, kept), jnp.where(odd, kept, came)]
        full = jnp.concatenate(rows_of, axis=0)
        tiles = [full[k * tile : (k + 1) * tile] for k in range(len(upper))]
        final = dict(zip(upper, tiles))
        diag = final[0, 0]
        for i in range(1, span):
            diag = diag + final[i, i]
        eye = lax.broadcasted_iota(jnp.int32, diag.shape, 0) == lax.broadcasted_iota(jnp.int32, diag.shape, 1)
        trace = jnp.sum(jnp.where(eye, diag, 0.0), keepdims=True)
        scale = width / trace
        for i, j in upper:
            value = final[i, j] * scale
            next_held[i * tile : (i + 1) * tile, j * tile : (j + 1) * tile] = value
            if i != j:
                next_held[j * tile : (j + 1) * tile, i * tile : (i + 1) * tile] = value.T
        next_copy = pltpu.make_async_copy(next_held, next_ref, sems.at[0])
        next_copy.start()
        mapped_held[...] = mul(left(points_ref[...]), right(next_held[...], axis=0))
        mapped_copy = pltpu.make_async_copy(mapped_held, mapped_ref, sems.at[1])
        mapped_copy.start()
        next_copy.wait()
        mapped_copy.wait()

    return pl.pallas_call(
        body,
        out_shape=(shape(width, width), shape(rows, width)),
        in_specs=[pl.BlockSpec(memory_space=pltpu.VMEM)] * 3,
        out_specs=(pl.BlockSpec(memory_space=pl.ANY),) * 2,
        scratch_shapes=[
            pltpu.VMEM((width, width), F32),
            pltpu.VMEM((rows, width), F32),
            pltpu.SemaphoreType.DMA((2,)),
        ],
        compiler_params=pltpu.CompilerParams(vmem_limit_bytes=40 * 1024 * 1024),
    )(keep, other, points)


def make_local(rows_all, cols_all):
    hop = make_hop(rows_all, cols_all)
    row_bits = bits_of(rows_all)
    col_bits = bits_of(cols_all)
    bit_a, bit_b = row_bits[0], row_bits[1]
    line_bits = row_bits[2:]

    def to_a(value):
        return hop(value, (bit_a, 0), (bit_b, 0))

    def to_b(value):
        return hop(value, (bit_b, 0), (bit_a, 0))

    def in_plane(parts):
        return [to_a(parts[0]), to_b(parts[1]), hop(parts[2], (bit_a | bit_b, 0))]

    def among(value, shifts):
        steps = [(0, 0)]
        for dr, dc in shifts:
            steps = steps + [(r | dr, c | dc) for r, c in steps]
        return [value] + [hop(value, step) for step in steps[1:]]

    def local(points, coeffs, metric):
        own, width = points.shape
        outs_n = coeffs.shape[1]
        points, packed = pack_own(points, coeffs)
        metric3 = metric_halves(metric)
        near = among(packed, [(bit, 0) for bit in reversed(line_bits)])
        late = [other for block in near for other in among(block, [(0, bit) for bit in col_bits])[1:]]
        source = copy_after(points, late[0])
        queries = [hop(source, (bit_a | bit_b, 0)), to_a(source), to_b(source), points]
        total, mapped = early_sums(queries[:2], near, metric3, outs_n)
        (part_ab,) = late_sums(queries[:1], 0, total, mapped, metric3, late, outs_n, queries[2:3])
        sent_ab = to_a(part_ab)
        (part_a,) = late_sums(queries[1:2], 1, total, mapped, metric3, late, outs_n)
        sent_a = to_a(part_a)
        part_b, part_own = whole_sums(queries[2:], near + late, metric3, outs_n)
        half_b = part_b + sent_ab
        rest_own = to_b(half_b)
        half_own = part_own + sent_a
        rest_b = to_b(half_own)

        mine, away = outer_quarters([half_own, rest_own, half_b, rest_b], metric3, rows_all)
        keep, send = split_halves(mine, to_a(away), rows_all)
        total = add_all([keep, hop(send, (0, 1))])
        for k in range(0, len(line_bits), 2):
            total = add_all(among(total, [(bit, 0) for bit in line_bits[k : k + 2]]))
        for bit in col_bits[1:]:
            total = add_all(among(total, [(0, bit)]))
        keep = join_quarters([total] + in_plane([total] * 3), rows_all)
        return finish(keep, hop(keep, (0, 1)), points, rows_all)

    return local


def solution(mesh):
    return jax.shard_map(
        make_local(mesh.shape["row"], mesh.shape["col"]),
        mesh=mesh,
        in_specs=(P(AXES, None), P(AXES, None), P()),
        out_specs=(P(), P(AXES, None)),
        check_vma=False,
    )
```

```python
import jax
import jax.numpy as jnp
from jax import lax
from jax.experimental import pallas as pl
from jax.experimental.pallas import tpu as pltpu
from jax.sharding import PartitionSpec as P

AXES = ("row", "col")
F32, BF16 = jnp.float32, jnp.bfloat16


def halves(x):
    high = x.astype(BF16)
    return high, (x - high.astype(F32)).astype(BF16)


def left(x, axis=1):
    high, low = halves(x)
    return jnp.concatenate([high, high, low], axis=axis)


def right(x, axis=1):
    high, low = halves(x)
    return jnp.concatenate([high, low, high], axis=axis)


def mul(a, b, da=1, db=0):
    return lax.dot_general(a, b, (((da,), (db,)), ((), ())), preferred_element_type=F32)


def round_up(count, step):
    return -(-count // step) * step


def bits_of(count):
    assert count & (count - 1) == 0
    return [1 << b for b in range(count.bit_length() - 1)]


def parity(x):
    return bin(x).count("1") & 1


def make_hop(rows, cols):
    def hop(value, even, odd=None):
        odd = even if odd is None else odd
        pairs = []
        for r in range(rows):
            for c in range(cols):
                dr, dc = odd if parity(r) ^ (c & 1) else even
                pairs.append((r * cols + c, (r ^ dr) * cols + (c ^ dc ^ parity(dr))))
        return lax.ppermute(value, AXES, pairs)

    return hop


def my_kind(rows):
    row, kind = lax.axis_index("row"), lax.axis_index("col")
    for bit in range(len(bits_of(rows))):
        kind = kind ^ (row >> bit)
    return kind & 1


def call(body, out_shape, args, flops):
    moved = sum(4 * a.size for a in args) + sum(4 * s.size for s in jax.tree.leaves(out_shape))
    return pl.pallas_call(
        body,
        out_shape=out_shape,
        in_specs=[pl.BlockSpec(memory_space=pltpu.VMEM)] * len(args),
        out_specs=jax.tree.map(lambda _: pl.BlockSpec(memory_space=pltpu.VMEM), out_shape),
        compiler_params=pltpu.CompilerParams(vmem_limit_bytes=40 * 1024 * 1024),
        cost_estimate=pl.CostEstimate(flops=flops, bytes_accessed=moved, transcendentals=0),
    )(*args)


def shape(*dims):
    return jax.ShapeDtypeStruct(dims, F32)


def pack_own(points, coeffs):
    rows, width = points.shape
    outs_n = coeffs.shape[1]
    extra = round_up(outs_n + 1, 8)

    def body(points_ref, cols_ref, plain_ref, packed_ref, cols_held, sems):
        copies = [
            pltpu.make_async_copy(points_ref, plain_ref, sems.at[0]),
            pltpu.make_async_copy(cols_ref, cols_held, sems.at[1]),
        ]
        for copy in copies:
            copy.start()
        packed_ref[rows:, :] = jnp.zeros((extra, width), F32)
        copies[1].wait()
        cols = cols_held[...]
        packed_ref[rows : rows + outs_n, 0 : 2 * rows] = jnp.concatenate([cols, cols], axis=1)
        copies[0].wait()
        packed_ref[0:rows, :] = plain_ref[...]

    return pl.pallas_call(
        body,
        out_shape=(pltpu.VMEM((rows, width), F32), pltpu.VMEM((rows + extra, width), F32)),
        in_specs=[pl.BlockSpec(memory_space=pl.ANY)] * 2,
        out_specs=(pl.BlockSpec(memory_space=pltpu.VMEM),) * 2,
        scratch_shapes=[pltpu.VMEM((outs_n, rows), F32), pltpu.SemaphoreType.DMA((2,))],
    )(points, coeffs.T)


def copy_after(value, wanted):
    def body(value_ref, wanted_ref, out_ref):
        out_ref[...] = value_ref[...]

    return call(body, shape(*value.shape), [value, wanted], 1)


def metric_halves(metric):
    high = lax.reduce_precision(metric, 8, 7)
    low = (metric - high).astype(BF16)
    return jnp.concatenate([high.astype(BF16), low, high.astype(BF16)], axis=0)


def norm_rows(centers, metric3, own):
    column = jnp.sum(centers * mul(left(centers), metric3), axis=1, keepdims=True)
    pair = 2 * own
    rows = [
        jnp.broadcast_to(column[k : k + pair], (pair, round_up(pair, 128))).T[0:1]
        for k in range(0, centers.shape[0], pair)
    ]
    return jnp.concatenate(rows, axis=1)


def center_terms(refs, own, outs_n, metric3):
    pieces, extras = [], []
    height = own + round_up(outs_n + 1, 8)
    for ref in refs:
        for first in range(0, ref.shape[0], height):
            pieces.append(ref[first : first + own, :])
            extras.append(ref[first + own : first + height, 0 : 2 * own])
    centers = jnp.concatenate(pieces, axis=0)
    lane = lax.broadcasted_iota(jnp.int32, extras[0].shape, 1)
    merged = [jnp.where(lane < own, extras[k], extras[k + 1]) for k in range(0, len(extras), 2)]
    rows = jnp.concatenate(merged, axis=1)
    return centers, norm_rows(centers, metric3, own), [rows[c : c + 1] for c in range(outs_n)]


def query_sums(query_x, query_y, centers, norm, coefs):
    query_n = jnp.sum(query_x * query_y, axis=1, keepdims=True)
    cross = mul(left(query_y), right(centers), 1, 1)
    distance = jnp.sqrt(jnp.maximum(query_n + norm - 2.0 * cross, 0.0))
    weights = jnp.exp(-distance) / jnp.maximum(distance, 0.5)
    low = centers.astype(BF16)
    parts = []
    for coef in coefs:
        scaled = weights * coef
        sums = jnp.sum(scaled, axis=1, keepdims=True)
        parts.append(sums * query_x - mul(scaled.astype(BF16), low))
    return parts


def chunks(refs):
    return [refs[k : k + 8] for k in range(0, len(refs), 8)]


def early_sums(queries, blocks, metric3, outs_n):
    own, width = queries[0].shape
    count = len(queries)

    def body(*refs):
        query_refs, block_refs = refs[:count], refs[count : count + len(blocks)]
        metric3_ref, total_ref, mapped_ref = refs[count + len(blocks) :]
        query_x = jnp.concatenate([ref[...] for ref in query_refs], axis=0)
        query_y = mul(left(query_x), metric3_ref[...])
        mapped_ref[...] = query_y
        for k, run in enumerate(chunks(block_refs)):
            parts = query_sums(query_x, query_y, *center_terms(run, own, outs_n, metric3_ref[...]))
            for c in range(outs_n):
                total_ref[c] = parts[c] if k == 0 else total_ref[c] + parts[c]

    args = list(queries) + list(blocks) + [metric3]
    centers = sum(b.shape[0] for b in blocks)
    flops = 6 * (count * own + centers) * width * width + 10 * count * own * centers * width
    return call(body, (shape(outs_n, count * own, width), shape(count * own, width)), args, flops)


def late_sums(queries, first, total, mapped, metric3, blocks, outs_n, wanted=()):
    own, width = queries[0].shape
    count = len(queries)

    def body(*refs):
        query_refs, block_refs = refs[:count], refs[count : count + len(blocks)]
        total_ref, mapped_ref, metric3_ref = refs[count + len(blocks) : count + len(blocks) + 3]
        out_refs = refs[count + len(blocks) + 3 + len(wanted) :]
        rows = slice(first * own, (first + count) * own)
        query_x = jnp.concatenate([ref[...] for ref in query_refs], axis=0)
        query_y = mapped_ref[rows, :]
        sums = [total_ref[c, rows, :] for c in range(outs_n)]
        for run in chunks(block_refs):
            terms = center_terms(run, own, outs_n, metric3_ref[...])
            sums = [a + b for a, b in zip(sums, query_sums(query_x, query_y, *terms))]
        for q in range(count):
            for c in range(outs_n):
                out_refs[q][c * own : (c + 1) * own, :] = sums[c][q * own : (q + 1) * own, :]

    args = list(queries) + list(blocks) + [total, mapped, metric3] + list(wanted)
    centers = sum(b.shape[0] for b in blocks)
    flops = 6 * centers * width * width + 10 * count * own * centers * width
    return call(body, tuple(shape(outs_n * own, width) for _ in queries), args, flops)


def whole_sums(queries, blocks, metric3, outs_n):
    own, width = queries[0].shape
    count = len(queries)

    def body(*refs):
        query_refs, block_refs = refs[:count], refs[count : count + len(blocks)]
        metric3_ref, out_refs = refs[count + len(blocks)], refs[count + len(blocks) + 1 :]
        query_x = jnp.concatenate([ref[...] for ref in query_refs], axis=0)
        query_y = mul(left(query_x), metric3_ref[...])
        sums = None
        for run in chunks(block_refs):
            parts = query_sums(query_x, query_y, *center_terms(run, own, outs_n, metric3_ref[...]))
            sums = parts if sums is None else [a + b for a, b in zip(sums, parts)]
        for q in range(count):
            for c in range(outs_n):
                out_refs[q][c * own : (c + 1) * own, :] = sums[c][q * own : (q + 1) * own, :]

    args = list(queries) + list(blocks) + [metric3]
    centers = sum(b.shape[0] for b in blocks)
    flops = 6 * (count * own + centers) * width * width + 10 * count * own * centers * width
    return call(body, tuple(shape(outs_n * own, width) for _ in queries), args, flops)


def upper_tiles(width):
    tile = 128 if width % 128 == 0 else width
    span = width // tile
    return tile, span, [(i, j) for i in range(span) for j in range(i, span)]


def outer_quarters(sums, metric3, rows_all):
    width = metric3.shape[1]
    tile, span, upper = upper_tiles(width)
    count = round_up(len(upper), 2)
    rows = count * tile // 4

    def body(*refs):
        metric3_ref, mine_ref, away_ref, full_ref = refs[len(sums) :]
        pairs = [refs[k][...] + refs[k + 1][...] for k in range(0, len(sums), 2)]
        grads = mul(left(jnp.concatenate(pairs, axis=0)), metric3_ref[...])
        grads_left, grads_right = left(grads, 0), right(grads, 0)
        for i in range(span):
            slab = mul(grads_left[:, i * tile : (i + 1) * tile], grads_right[:, i * tile :], 0, 0)
            for j in range(i, span):
                row = upper.index((i, j)) * tile
                full_ref[row : row + tile, :] = slab[:, (j - i) * tile : (j - i + 1) * tile]
        if count > len(upper):
            full_ref[len(upper) * tile :, :] = jnp.zeros(((count - len(upper)) * tile, tile), F32)
        for k, out_ref in enumerate([mine_ref, away_ref]):
            out_ref[...] = full_ref[quarter(full_ref, k, rows_all), :]

    out = shape(rows, tile)
    return pl.pallas_call(
        body,
        out_shape=(out, out),
        in_specs=[pl.BlockSpec(memory_space=pltpu.VMEM)] * (len(sums) + 1),
        out_specs=(pl.BlockSpec(memory_space=pltpu.VMEM),) * 2,
        scratch_shapes=[pltpu.VMEM((count * tile, tile), F32)],
        compiler_params=pltpu.CompilerParams(vmem_limit_bytes=40 * 1024 * 1024),
    )(*sums, metric3)


def plane_place(k, rows_all):
    row = lax.axis_index("row") & 3
    if k in (1, 2):
        return row ^ jnp.where(my_kind(rows_all) == 1, 3 - k, k)
    return row ^ k


def quarter(ref, k, rows_all):
    rows = ref.shape[0] // 4
    return pl.ds(pl.multiple_of(plane_place(k, rows_all) * rows, rows), rows)


def split_halves(mine, arrived, rows_all):
    rows, width = mine.shape
    half = rows // 2

    def body(mine_ref, arrived_ref, keep_ref, send_ref):
        kind = my_kind(rows_all)
        for place, out_ref in ((kind, keep_ref), (1 - kind, send_ref)):
            here = pl.ds(pl.multiple_of(place * half, half), half)
            out_ref[...] = mine_ref[here, :] + arrived_ref[here, :]

    return call(body, (shape(half, width),) * 2, [mine, arrived], 1)


def join_quarters(parts, rows_all):
    rows, width = parts[0].shape

    def body(*refs):
        out_ref = refs[-1]
        for k in range(4):
            out_ref[quarter(out_ref, k, rows_all), :] = refs[k][...]

    return call(body, shape(4 * rows, width), parts, 1)


def add_all(parts):
    def body(*refs):
        values = [ref[...] for ref in refs[:-1]]
        while len(values) > 1:
            values = [a + b for a, b in zip(values[::2], values[1::2])]
        refs[-1][...] = values[0]

    return call(body, shape(*parts[0].shape), parts, 1)


def finish(keep, other, points, rows_all):
    rows, width = points.shape
    tile, span, upper = upper_tiles(width)

    def body(keep_ref, other_ref, points_ref, next_ref, mapped_ref, next_held, mapped_held, sems):
        odd = my_kind(rows_all) == 1
        piece = keep_ref.shape[0] // 4
        rows_of = []
        for k in range(4):
            kept, came = (ref[k * piece : (k + 1) * piece, :] for ref in (keep_ref, other_ref))
            rows_of += [jnp.where(odd, came, kept), jnp.where(odd, kept, came)]
        full = jnp.concatenate(rows_of, axis=0)
        tiles = [full[k * tile : (k + 1) * tile] for k in range(len(upper))]
        final = dict(zip(upper, tiles))
        diag = final[0, 0]
        for i in range(1, span):
            diag = diag + final[i, i]
        eye = lax.broadcasted_iota(jnp.int32, diag.shape, 0) == lax.broadcasted_iota(jnp.int32, diag.shape, 1)
        trace = jnp.sum(jnp.where(eye, diag, 0.0), keepdims=True)
        scale = width / trace
        for i, j in upper:
            value = final[i, j] * scale
            next_held[i * tile : (i + 1) * tile, j * tile : (j + 1) * tile] = value
            if i != j:
                next_held[j * tile : (j + 1) * tile, i * tile : (i + 1) * tile] = value.T
        next_copy = pltpu.make_async_copy(next_held, next_ref, sems.at[0])
        next_copy.start()
        mapped_held[...] = mul(left(points_ref[...]), right(next_held[...], axis=0))
        mapped_copy = pltpu.make_async_copy(mapped_held, mapped_ref, sems.at[1])
        mapped_copy.start()
        next_copy.wait()
        mapped_copy.wait()

    return pl.pallas_call(
        body,
        out_shape=(shape(width, width), shape(rows, width)),
        in_specs=[pl.BlockSpec(memory_space=pltpu.VMEM)] * 3,
        out_specs=(pl.BlockSpec(memory_space=pl.ANY),) * 2,
        scratch_shapes=[
            pltpu.VMEM((width, width), F32),
            pltpu.VMEM((rows, width), F32),
            pltpu.SemaphoreType.DMA((2,)),
        ],
        compiler_params=pltpu.CompilerParams(vmem_limit_bytes=40 * 1024 * 1024),
    )(keep, other, points)


def make_local(rows_all, cols_all):
    hop = make_hop(rows_all, cols_all)
    row_bits = bits_of(rows_all)
    col_bits = bits_of(cols_all)
    bit_a, bit_b = row_bits[0], row_bits[1]
    line_bits = row_bits[2:]

    def to_a(value):
        return hop(value, (bit_a, 0), (bit_b, 0))

    def to_b(value):
        return hop(value, (bit_b, 0), (bit_a, 0))

    def in_plane(parts):
        return [to_a(parts[0]), to_b(parts[1]), hop(parts[2], (bit_a | bit_b, 0))]

    def among(value, shifts):
        steps = [(0, 0)]
        for dr, dc in shifts:
            steps = steps + [(r | dr, c | dc) for r, c in steps]
        return [value] + [hop(value, step) for step in steps[1:]]

    def local(points, coeffs, metric):
        own, width = points.shape
        outs_n = coeffs.shape[1]
        points, packed = pack_own(points, coeffs)
        metric3 = metric_halves(metric)
        near = among(packed, [(bit, 0) for bit in reversed(line_bits)])
        near = near[:1] + near[:0:-1]
        late = [other for block in near for other in among(block, [(0, bit) for bit in col_bits])[1:]]
        source = copy_after(points, late[0])
        queries = [hop(source, (bit_a | bit_b, 0)), to_a(source), to_b(source), points]
        total, mapped = early_sums(queries[:2], near, metric3, outs_n)
        (part_ab,) = late_sums(queries[:1], 0, total, mapped, metric3, late, outs_n, queries[2:3])
        sent_ab = to_a(part_ab)
        (part_a,) = late_sums(queries[1:2], 1, total, mapped, metric3, late, outs_n)
        sent_a = to_a(part_a)
        part_b, part_own = whole_sums(queries[2:], near + late, metric3, outs_n)
        half_b = part_b + sent_ab
        rest_own = to_b(half_b)
        half_own = part_own + sent_a
        rest_b = to_b(half_own)

        mine, away = outer_quarters([half_own, rest_own, half_b, rest_b], metric3, rows_all)
        keep, send = split_halves(mine, to_a(away), rows_all)
        total = add_all([keep, hop(send, (0, 1))])
        for k in range(0, len(line_bits), 2):
            total = add_all(among(total, [(bit, 0) for bit in line_bits[k : k + 2]]))
        for bit in col_bits[1:]:
            total = add_all(among(total, [(0, bit)]))
        keep = join_quarters([total] + in_plane([total] * 3), rows_all)
        return finish(keep, hop(keep, (0, 1)), points, rows_all)

    return local


def solution(mesh):
    return jax.shard_map(
        make_local(mesh.shape["row"], mesh.shape["col"]),
        mesh=mesh,
        in_specs=(P(AXES, None), P(AXES, None), P()),
        out_specs=(P(), P(AXES, None)),
        check_vma=False,
    )
```

```python
import jax
import jax.numpy as jnp
from jax import lax
from jax.experimental import pallas as pl
from jax.experimental.pallas import tpu as pltpu
from jax.sharding import PartitionSpec as P

AXES = ("row", "col")
F32, BF16 = jnp.float32, jnp.bfloat16


def halves(x):
    high = x.astype(BF16)
    return high, (x - high.astype(F32)).astype(BF16)


def left(x, axis=1):
    high, low = halves(x)
    return jnp.concatenate([high, high, low], axis=axis)


def right(x, axis=1):
    high, low = halves(x)
    return jnp.concatenate([high, low, high], axis=axis)


def mul(a, b, da=1, db=0):
    return lax.dot_general(a, b, (((da,), (db,)), ((), ())), preferred_element_type=F32)


def round_up(count, step):
    return -(-count // step) * step


def bits_of(count):
    assert count & (count - 1) == 0
    return [1 << b for b in range(count.bit_length() - 1)]


def parity(x):
    return bin(x).count("1") & 1


def make_hop(rows, cols):
    def hop(value, even, odd=None):
        odd = even if odd is None else odd
        pairs = []
        for r in range(rows):
            for c in range(cols):
                dr, dc = odd if parity(r) ^ (c & 1) else even
                pairs.append((r * cols + c, (r ^ dr) * cols + (c ^ dc ^ parity(dr))))
        return lax.ppermute(value, AXES, pairs)

    return hop


def my_kind(rows):
    row, kind = lax.axis_index("row"), lax.axis_index("col")
    for bit in range(len(bits_of(rows))):
        kind = kind ^ (row >> bit)
    return kind & 1


def call(body, out_shape, args, flops):
    moved = sum(4 * a.size for a in args) + sum(4 * s.size for s in jax.tree.leaves(out_shape))
    return pl.pallas_call(
        body,
        out_shape=out_shape,
        in_specs=[pl.BlockSpec(memory_space=pltpu.VMEM)] * len(args),
        out_specs=jax.tree.map(lambda _: pl.BlockSpec(memory_space=pltpu.VMEM), out_shape),
        compiler_params=pltpu.CompilerParams(vmem_limit_bytes=40 * 1024 * 1024),
        cost_estimate=pl.CostEstimate(flops=flops, bytes_accessed=moved, transcendentals=0),
    )(*args)


def shape(*dims):
    return jax.ShapeDtypeStruct(dims, F32)


def pack_own(points, coeffs):
    rows, width = points.shape
    outs_n = coeffs.shape[1]
    extra = round_up(outs_n + 1, 8)

    def body(points_ref, cols_ref, plain_ref, packed_ref, cols_held, sems):
        copies = [
            pltpu.make_async_copy(points_ref, plain_ref, sems.at[0]),
            pltpu.make_async_copy(cols_ref, cols_held, sems.at[1]),
        ]
        for copy in copies:
            copy.start()
        packed_ref[rows:, :] = jnp.zeros((extra, width), F32)
        copies[1].wait()
        cols = cols_held[...]
        packed_ref[rows : rows + outs_n, 0 : 2 * rows] = jnp.concatenate([cols, cols], axis=1)
        copies[0].wait()
        packed_ref[0:rows, :] = plain_ref[...]

    return pl.pallas_call(
        body,
        out_shape=(pltpu.VMEM((rows, width), F32), pltpu.VMEM((rows + extra, width), F32)),
        in_specs=[pl.BlockSpec(memory_space=pl.ANY)] * 2,
        out_specs=(pl.BlockSpec(memory_space=pltpu.VMEM),) * 2,
        scratch_shapes=[pltpu.VMEM((outs_n, rows), F32), pltpu.SemaphoreType.DMA((2,))],
    )(points, coeffs.T)


def copy_after(value, wanted):
    def body(value_ref, wanted_ref, out_ref):
        out_ref[...] = value_ref[...]

    return call(body, shape(*value.shape), [value, wanted], 1)


def metric_halves(metric):
    high = lax.reduce_precision(metric, 8, 7)
    low = (metric - high).astype(BF16)
    return jnp.concatenate([high.astype(BF16), low, high.astype(BF16)], axis=0)


def norm_rows(centers, metric3, own):
    column = jnp.sum(centers * mul(left(centers), metric3), axis=1, keepdims=True)
    pair = 2 * own
    rows = [
        jnp.broadcast_to(column[k : k + pair], (pair, round_up(pair, 128))).T[0:1]
        for k in range(0, centers.shape[0], pair)
    ]
    return jnp.concatenate(rows, axis=1)


def center_terms(refs, own, outs_n, metric3):
    pieces, extras = [], []
    height = own + round_up(outs_n + 1, 8)
    for ref in refs:
        for first in range(0, ref.shape[0], height):
            pieces.append(ref[first : first + own, :])
            extras.append(ref[first + own : first + height, 0 : 2 * own])
    centers = jnp.concatenate(pieces, axis=0)
    lane = lax.broadcasted_iota(jnp.int32, extras[0].shape, 1)
    merged = [jnp.where(lane < own, extras[k], extras[k + 1]) for k in range(0, len(extras), 2)]
    rows = jnp.concatenate(merged, axis=1)
    return centers, norm_rows(centers, metric3, own), [rows[c : c + 1] for c in range(outs_n)]


def query_sums(query_x, query_y, centers, norm, coefs):
    query_n = jnp.sum(query_x * query_y, axis=1, keepdims=True)
    cross = mul(left(query_y), right(centers), 1, 1)
    distance = jnp.sqrt(jnp.maximum(query_n + norm - 2.0 * cross, 0.0))
    weights = jnp.exp(-distance) / jnp.maximum(distance, 0.5)
    low = centers.astype(BF16)
    parts = []
    for coef in coefs:
        scaled = weights * coef
        sums = jnp.sum(scaled, axis=1, keepdims=True)
        parts.append(sums * query_x - mul(scaled.astype(BF16), low))
    return parts


def chunks(refs):
    return [refs[k : k + 8] for k in range(0, len(refs), 8)]


def early_sums(queries, blocks, metric3, outs_n):
    own, width = queries[0].shape
    count = len(queries)

    def body(*refs):
        query_refs, block_refs = refs[:count], refs[count : count + len(blocks)]
        metric3_ref, total_ref, mapped_ref = refs[count + len(blocks) :]
        query_x = jnp.concatenate([ref[...] for ref in query_refs], axis=0)
        query_y = mul(left(query_x), metric3_ref[...])
        mapped_ref[...] = query_y
        for k, run in enumerate(chunks(block_refs)):
            parts = query_sums(query_x, query_y, *center_terms(run, own, outs_n, metric3_ref[...]))
            for c in range(outs_n):
                total_ref[c] = parts[c] if k == 0 else total_ref[c] + parts[c]

    args = list(queries) + list(blocks) + [metric3]
    centers = sum(b.shape[0] for b in blocks)
    flops = 6 * (count * own + centers) * width * width + 10 * count * own * centers * width
    return call(body, (shape(outs_n, count * own, width), shape(count * own, width)), args, flops)


def late_sums(queries, first, total, mapped, metric3, blocks, outs_n, wanted=()):
    own, width = queries[0].shape
    count = len(queries)

    def body(*refs):
        query_refs, block_refs = refs[:count], refs[count : count + len(blocks)]
        total_ref, mapped_ref, metric3_ref = refs[count + len(blocks) : count + len(blocks) + 3]
        out_refs = refs[count + len(blocks) + 3 + len(wanted) :]
        rows = slice(first * own, (first + count) * own)
        query_x = jnp.concatenate([ref[...] for ref in query_refs], axis=0)
        query_y = mapped_ref[rows, :]
        sums = [total_ref[c, rows, :] for c in range(outs_n)]
        for run in chunks(block_refs):
            terms = center_terms(run, own, outs_n, metric3_ref[...])
            sums = [a + b for a, b in zip(sums, query_sums(query_x, query_y, *terms))]
        for q in range(count):
            for c in range(outs_n):
                out_refs[q][c * own : (c + 1) * own, :] = sums[c][q * own : (q + 1) * own, :]

    args = list(queries) + list(blocks) + [total, mapped, metric3] + list(wanted)
    centers = sum(b.shape[0] for b in blocks)
    flops = 6 * centers * width * width + 10 * count * own * centers * width
    return call(body, tuple(shape(outs_n * own, width) for _ in queries), args, flops)


def whole_sums(queries, blocks, metric3, outs_n):
    own, width = queries[0].shape
    count = len(queries)

    def body(*refs):
        query_refs, block_refs = refs[:count], refs[count : count + len(blocks)]
        metric3_ref, out_refs = refs[count + len(blocks)], refs[count + len(blocks) + 1 :]
        query_x = jnp.concatenate([ref[...] for ref in query_refs], axis=0)
        query_y = mul(left(query_x), metric3_ref[...])
        sums = None
        for run in chunks(block_refs):
            parts = query_sums(query_x, query_y, *center_terms(run, own, outs_n, metric3_ref[...]))
            sums = parts if sums is None else [a + b for a, b in zip(sums, parts)]
        for q in range(count):
            for c in range(outs_n):
                out_refs[q][c * own : (c + 1) * own, :] = sums[c][q * own : (q + 1) * own, :]

    args = list(queries) + list(blocks) + [metric3]
    centers = sum(b.shape[0] for b in blocks)
    flops = 6 * (count * own + centers) * width * width + 10 * count * own * centers * width
    return call(body, tuple(shape(outs_n * own, width) for _ in queries), args, flops)


def upper_tiles(width):
    tile = 128 if width % 128 == 0 else width
    span = width // tile
    return tile, span, [(i, j) for i in range(span) for j in range(i, span)]


def outer_quarters(sums, metric3, rows_all):
    width = metric3.shape[1]
    tile, span, upper = upper_tiles(width)
    count = round_up(len(upper), 2)
    rows = count * tile // 4

    def body(*refs):
        metric3_ref, mine_ref, away_ref, full_ref = refs[len(sums) :]
        pairs = [refs[k][...] + refs[k + 1][...] for k in range(0, len(sums), 2)]
        grads = mul(left(jnp.concatenate(pairs, axis=0)), metric3_ref[...])
        grads_left, grads_right = left(grads, 0), right(grads, 0)
        for i in range(span):
            slab = mul(grads_left[:, i * tile : (i + 1) * tile], grads_right[:, i * tile :], 0, 0)
            for j in range(i, span):
                row = upper.index((i, j)) * tile
                full_ref[row : row + tile, :] = slab[:, (j - i) * tile : (j - i + 1) * tile]
        if count > len(upper):
            full_ref[len(upper) * tile :, :] = jnp.zeros(((count - len(upper)) * tile, tile), F32)
        for k, out_ref in enumerate([mine_ref, away_ref]):
            out_ref[...] = full_ref[quarter(full_ref, k, rows_all), :]

    out = shape(rows, tile)
    return pl.pallas_call(
        body,
        out_shape=(out, out),
        in_specs=[pl.BlockSpec(memory_space=pltpu.VMEM)] * (len(sums) + 1),
        out_specs=(pl.BlockSpec(memory_space=pltpu.VMEM),) * 2,
        scratch_shapes=[pltpu.VMEM((count * tile, tile), F32)],
        compiler_params=pltpu.CompilerParams(vmem_limit_bytes=40 * 1024 * 1024),
    )(*sums, metric3)


def plane_place(k, rows_all):
    row = lax.axis_index("row") & 3
    if k in (1, 2):
        return row ^ jnp.where(my_kind(rows_all) == 1, 3 - k, k)
    return row ^ k


def quarter(ref, k, rows_all):
    rows = ref.shape[0] // 4
    return pl.ds(pl.multiple_of(plane_place(k, rows_all) * rows, rows), rows)


def split_halves(mine, arrived, rows_all):
    rows, width = mine.shape
    half = rows // 2

    def body(mine_ref, arrived_ref, keep_ref, send_ref):
        kind = my_kind(rows_all)
        for place, out_ref in ((kind, keep_ref), (1 - kind, send_ref)):
            here = pl.ds(pl.multiple_of(place * half, half), half)
            out_ref[...] = mine_ref[here, :] + arrived_ref[here, :]

    return call(body, (shape(half, width),) * 2, [mine, arrived], 1)


def join_quarters(parts, rows_all):
    rows, width = parts[0].shape

    def body(*refs):
        out_ref = refs[-1]
        for k in range(4):
            out_ref[quarter(out_ref, k, rows_all), :] = refs[k][...]

    return call(body, shape(4 * rows, width), parts, 1)


def add_all(parts):
    def body(*refs):
        values = [ref[...] for ref in refs[:-1]]
        while len(values) > 1:
            values = [a + b for a, b in zip(values[::2], values[1::2])]
        refs[-1][...] = values[0]

    return call(body, shape(*parts[0].shape), parts, 1)


def finish(keep, other, points, rows_all):
    rows, width = points.shape
    tile, span, upper = upper_tiles(width)

    def body(keep_ref, other_ref, points_ref, next_ref, mapped_ref, next_held, mapped_held, sems):
        odd = my_kind(rows_all) == 1
        piece = keep_ref.shape[0] // 4
        rows_of = []
        for k in range(4):
            kept, came = (ref[k * piece : (k + 1) * piece, :] for ref in (keep_ref, other_ref))
            rows_of += [jnp.where(odd, came, kept), jnp.where(odd, kept, came)]
        full = jnp.concatenate(rows_of, axis=0)
        tiles = [full[k * tile : (k + 1) * tile] for k in range(len(upper))]
        final = dict(zip(upper, tiles))
        diag = final[0, 0]
        for i in range(1, span):
            diag = diag + final[i, i]
        eye = lax.broadcasted_iota(jnp.int32, diag.shape, 0) == lax.broadcasted_iota(jnp.int32, diag.shape, 1)
        trace = jnp.sum(jnp.where(eye, diag, 0.0), keepdims=True)
        scale = width / trace
        for i, j in upper:
            value = final[i, j] * scale
            next_held[i * tile : (i + 1) * tile, j * tile : (j + 1) * tile] = value
            if i != j:
                next_held[j * tile : (j + 1) * tile, i * tile : (i + 1) * tile] = value.T
        next_copy = pltpu.make_async_copy(next_held, next_ref, sems.at[0])
        next_copy.start()
        mapped_held[...] = mul(left(points_ref[...]), right(next_held[...], axis=0))
        mapped_copy = pltpu.make_async_copy(mapped_held, mapped_ref, sems.at[1])
        mapped_copy.start()
        next_copy.wait()
        mapped_copy.wait()

    return pl.pallas_call(
        body,
        out_shape=(shape(width, width), shape(rows, width)),
        in_specs=[pl.BlockSpec(memory_space=pltpu.VMEM)] * 3,
        out_specs=(pl.BlockSpec(memory_space=pl.ANY),) * 2,
        scratch_shapes=[
            pltpu.VMEM((width, width), F32),
            pltpu.VMEM((rows, width), F32),
            pltpu.SemaphoreType.DMA((2,)),
        ],
        compiler_params=pltpu.CompilerParams(vmem_limit_bytes=40 * 1024 * 1024),
    )(keep, other, points)


def make_local(rows_all, cols_all):
    hop = make_hop(rows_all, cols_all)
    row_bits = bits_of(rows_all)
    col_bits = bits_of(cols_all)
    bit_a, bit_b = row_bits[0], row_bits[1]
    line_bits = row_bits[2:]

    def to_a(value):
        return hop(value, (bit_a, 0), (bit_b, 0))

    def to_b(value):
        return hop(value, (bit_b, 0), (bit_a, 0))

    def in_plane(parts):
        return [to_a(parts[0]), to_b(parts[1]), hop(parts[2], (bit_a | bit_b, 0))]

    def among(value, shifts):
        steps = [(0, 0)]
        for dr, dc in shifts:
            steps = steps + [(r | dr, c | dc) for r, c in steps]
        return [value] + [hop(value, step) for step in steps[1:]]

    def local(points, coeffs, metric):
        own, width = points.shape
        outs_n = coeffs.shape[1]
        points, packed = pack_own(points, coeffs)
        metric3 = metric_halves(metric)
        near = among(packed, [(bit, 0) for bit in reversed(line_bits)])
        near = near[:1] + near[:0:-1]
        across = [among(block, [(0, bit) for bit in col_bits])[1:] for block in near]
        first, late = across[0] + across[-1], [other for blocks in across[1:-1] for other in blocks]
        source = copy_after(points, first[0])
        queries = [hop(source, (bit_a | bit_b, 0)), to_a(source), to_b(source), points]
        total, mapped = early_sums(queries[:2], near + first, metric3, outs_n)
        (part_ab,) = late_sums(queries[:1], 0, total, mapped, metric3, late, outs_n, queries[2:3])
        sent_ab = to_a(part_ab)
        (part_a,) = late_sums(queries[1:2], 1, total, mapped, metric3, late, outs_n)
        sent_a = to_a(part_a)
        part_b, part_own = whole_sums(queries[2:], near + first + late, metric3, outs_n)
        half_b = part_b + sent_ab
        rest_own = to_b(half_b)
        half_own = part_own + sent_a
        rest_b = to_b(half_own)

        mine, away = outer_quarters([half_own, rest_own, half_b, rest_b], metric3, rows_all)
        keep, send = split_halves(mine, to_a(away), rows_all)
        total = add_all([keep, hop(send, (0, 1))])
        for k in range(0, len(line_bits), 2):
            total = add_all(among(total, [(bit, 0) for bit in line_bits[k : k + 2]]))
        for bit in col_bits[1:]:
            total = add_all(among(total, [(0, bit)]))
        keep = join_quarters([total] + in_plane([total] * 3), rows_all)
        return finish(keep, hop(keep, (0, 1)), points, rows_all)

    return local


def solution(mesh):
    return jax.shard_map(
        make_local(mesh.shape["row"], mesh.shape["col"]),
        mesh=mesh,
        in_specs=(P(AXES, None), P(AXES, None), P()),
        out_specs=(P(), P(AXES, None)),
        check_vma=False,
    )
```

```python
import jax
import jax.numpy as jnp
from jax import lax
from jax.experimental import pallas as pl
from jax.experimental.pallas import tpu as pltpu
from jax.sharding import PartitionSpec as P

AXES = ("row", "col")
F32, BF16 = jnp.float32, jnp.bfloat16


def halves(x):
    high = x.astype(BF16)
    return high, (x - high.astype(F32)).astype(BF16)


def left(x, axis=1):
    high, low = halves(x)
    return jnp.concatenate([high, high, low], axis=axis)


def right(x, axis=1):
    high, low = halves(x)
    return jnp.concatenate([high, low, high], axis=axis)


def mul(a, b, da=1, db=0):
    return lax.dot_general(a, b, (((da,), (db,)), ((), ())), preferred_element_type=F32)


def round_up(count, step):
    return -(-count // step) * step


def bits_of(count):
    assert count & (count - 1) == 0
    return [1 << b for b in range(count.bit_length() - 1)]


def parity(x):
    return bin(x).count("1") & 1


def make_hop(rows, cols):
    def hop(value, even, odd=None):
        odd = even if odd is None else odd
        pairs = []
        for r in range(rows):
            for c in range(cols):
                dr, dc = odd if parity(r) ^ (c & 1) else even
                pairs.append((r * cols + c, (r ^ dr) * cols + (c ^ dc ^ parity(dr))))
        return lax.ppermute(value, AXES, pairs)

    return hop


def my_kind(rows):
    row, kind = lax.axis_index("row"), lax.axis_index("col")
    for bit in range(len(bits_of(rows))):
        kind = kind ^ (row >> bit)
    return kind & 1


def call(body, out_shape, args, flops):
    moved = sum(4 * a.size for a in args) + sum(4 * s.size for s in jax.tree.leaves(out_shape))
    return pl.pallas_call(
        body,
        out_shape=out_shape,
        in_specs=[pl.BlockSpec(memory_space=pltpu.VMEM)] * len(args),
        out_specs=jax.tree.map(lambda _: pl.BlockSpec(memory_space=pltpu.VMEM), out_shape),
        compiler_params=pltpu.CompilerParams(vmem_limit_bytes=40 * 1024 * 1024),
        cost_estimate=pl.CostEstimate(flops=flops, bytes_accessed=moved, transcendentals=0),
    )(*args)


def shape(*dims):
    return jax.ShapeDtypeStruct(dims, F32)


def pack_own(points, coeffs):
    rows, width = points.shape
    outs_n = coeffs.shape[1]
    extra = round_up(outs_n + 1, 8)

    def body(points_ref, cols_ref, plain_ref, packed_ref, cols_held, sems):
        copies = [
            pltpu.make_async_copy(points_ref, plain_ref, sems.at[0]),
            pltpu.make_async_copy(cols_ref, cols_held, sems.at[1]),
        ]
        for copy in copies:
            copy.start()
        packed_ref[rows:, :] = jnp.zeros((extra, width), F32)
        copies[1].wait()
        cols = cols_held[...]
        packed_ref[rows : rows + outs_n, 0 : 2 * rows] = jnp.concatenate([cols, cols], axis=1)
        copies[0].wait()
        packed_ref[0:rows, :] = plain_ref[...]

    return pl.pallas_call(
        body,
        out_shape=(pltpu.VMEM((rows, width), F32), pltpu.VMEM((rows + extra, width), F32)),
        in_specs=[pl.BlockSpec(memory_space=pl.ANY)] * 2,
        out_specs=(pl.BlockSpec(memory_space=pltpu.VMEM),) * 2,
        scratch_shapes=[pltpu.VMEM((outs_n, rows), F32), pltpu.SemaphoreType.DMA((2,))],
    )(points, coeffs.T)


def copy_after(value, wanted):
    def body(value_ref, wanted_ref, out_ref):
        out_ref[...] = value_ref[...]

    return call(body, shape(*value.shape), [value, wanted], 1)


def metric_halves(metric):
    high = lax.reduce_precision(metric, 8, 7)
    low = (metric - high).astype(BF16)
    return jnp.concatenate([high.astype(BF16), low, high.astype(BF16)], axis=0)


def norm_rows(centers, metric3, own):
    column = jnp.sum(centers * mul(left(centers), metric3), axis=1, keepdims=True)
    pair = 2 * own
    rows = [
        jnp.broadcast_to(column[k : k + pair], (pair, round_up(pair, 128))).T[0:1]
        for k in range(0, centers.shape[0], pair)
    ]
    return jnp.concatenate(rows, axis=1)


def center_terms(refs, own, outs_n, metric3):
    pieces, extras = [], []
    height = own + round_up(outs_n + 1, 8)
    for ref in refs:
        for first in range(0, ref.shape[0], height):
            pieces.append(ref[first : first + own, :])
            extras.append(ref[first + own : first + height, 0 : 2 * own])
    centers = jnp.concatenate(pieces, axis=0)
    lane = lax.broadcasted_iota(jnp.int32, extras[0].shape, 1)
    merged = [jnp.where(lane < own, extras[k], extras[k + 1]) for k in range(0, len(extras), 2)]
    rows = jnp.concatenate(merged, axis=1)
    return centers, norm_rows(centers, metric3, own), [rows[c : c + 1] for c in range(outs_n)]


def query_sums(query_x, query_y, centers, norm, coefs):
    query_n = jnp.sum(query_x * query_y, axis=1, keepdims=True)
    cross = mul(left(query_y), right(centers), 1, 1)
    distance = jnp.sqrt(jnp.maximum(query_n + norm - 2.0 * cross, 0.0))
    weights = jnp.exp(-distance) / jnp.maximum(distance, 0.5)
    low = centers.astype(BF16)
    parts = []
    for coef in coefs:
        scaled = weights * coef
        sums = jnp.sum(scaled, axis=1, keepdims=True)
        parts.append(sums * query_x - mul(scaled.astype(BF16), low))
    return parts


def chunks(refs):
    return [refs[k : k + 8] for k in range(0, len(refs), 8)]


def early_sums(queries, blocks, metric3, outs_n):
    own, width = queries[0].shape
    count = len(queries)

    def body(*refs):
        query_refs, block_refs = refs[:count], refs[count : count + len(blocks)]
        metric3_ref, total_ref, mapped_ref = refs[count + len(blocks) :]
        query_x = jnp.concatenate([ref[...] for ref in query_refs], axis=0)
        query_y = mul(left(query_x), metric3_ref[...])
        mapped_ref[...] = query_y
        for k, run in enumerate(chunks(block_refs)):
            parts = query_sums(query_x, query_y, *center_terms(run, own, outs_n, metric3_ref[...]))
            for c in range(outs_n):
                total_ref[c] = parts[c] if k == 0 else total_ref[c] + parts[c]

    args = list(queries) + list(blocks) + [metric3]
    centers = sum(b.shape[0] for b in blocks)
    flops = 6 * (count * own + centers) * width * width + 10 * count * own * centers * width
    return call(body, (shape(outs_n, count * own, width), shape(count * own, width)), args, flops)


def late_sums(queries, first, total, mapped, metric3, blocks, outs_n, wanted=()):
    own, width = queries[0].shape
    count = len(queries)

    def body(*refs):
        query_refs, block_refs = refs[:count], refs[count : count + len(blocks)]
        total_ref, mapped_ref, metric3_ref = refs[count + len(blocks) : count + len(blocks) + 3]
        out_refs = refs[count + len(blocks) + 3 + len(wanted) :]
        rows = slice(first * own, (first + count) * own)
        query_x = jnp.concatenate([ref[...] for ref in query_refs], axis=0)
        query_y = mapped_ref[rows, :]
        sums = [total_ref[c, rows, :] for c in range(outs_n)]
        for run in chunks(block_refs):
            terms = center_terms(run, own, outs_n, metric3_ref[...])
            sums = [a + b for a, b in zip(sums, query_sums(query_x, query_y, *terms))]
        for q in range(count):
            for c in range(outs_n):
                out_refs[q][c * own : (c + 1) * own, :] = sums[c][q * own : (q + 1) * own, :]

    args = list(queries) + list(blocks) + [total, mapped, metric3] + list(wanted)
    centers = sum(b.shape[0] for b in blocks)
    flops = 6 * centers * width * width + 10 * count * own * centers * width
    return call(body, tuple(shape(outs_n * own, width) for _ in queries), args, flops)


def whole_sums(queries, blocks, metric3, outs_n):
    own, width = queries[0].shape
    count = len(queries)

    def body(*refs):
        query_refs, block_refs = refs[:count], refs[count : count + len(blocks)]
        metric3_ref, out_refs = refs[count + len(blocks)], refs[count + len(blocks) + 1 :]
        query_x = jnp.concatenate([ref[...] for ref in query_refs], axis=0)
        query_y = mul(left(query_x), metric3_ref[...])
        sums = None
        for run in chunks(block_refs):
            parts = query_sums(query_x, query_y, *center_terms(run, own, outs_n, metric3_ref[...]))
            sums = parts if sums is None else [a + b for a, b in zip(sums, parts)]
        for q in range(count):
            for c in range(outs_n):
                out_refs[q][c * own : (c + 1) * own, :] = sums[c][q * own : (q + 1) * own, :]

    args = list(queries) + list(blocks) + [metric3]
    centers = sum(b.shape[0] for b in blocks)
    flops = 6 * (count * own + centers) * width * width + 10 * count * own * centers * width
    return call(body, tuple(shape(outs_n * own, width) for _ in queries), args, flops)


def upper_tiles(width):
    tile = 128 if width % 128 == 0 else width
    span = width // tile
    return tile, span, [(i, j) for i in range(span) for j in range(i, span)]


def outer_quarters(sums, metric3, rows_all):
    width = metric3.shape[1]
    tile, span, upper = upper_tiles(width)
    count = round_up(len(upper), 2)
    rows = count * tile // 4

    def body(*refs):
        metric3_ref, mine_ref, away_ref, full_ref = refs[len(sums) :]
        pairs = [refs[k][...] + refs[k + 1][...] for k in range(0, len(sums), 2)]
        grads = mul(left(jnp.concatenate(pairs, axis=0)), metric3_ref[...])
        grads_left, grads_right = left(grads, 0), right(grads, 0)
        for i in range(span):
            slab = mul(grads_left[:, i * tile : (i + 1) * tile], grads_right[:, i * tile :], 0, 0)
            for j in range(i, span):
                row = upper.index((i, j)) * tile
                full_ref[row : row + tile, :] = slab[:, (j - i) * tile : (j - i + 1) * tile]
        if count > len(upper):
            full_ref[len(upper) * tile :, :] = jnp.zeros(((count - len(upper)) * tile, tile), F32)
        for k, out_ref in enumerate([mine_ref, away_ref]):
            out_ref[...] = full_ref[quarter(full_ref, k, rows_all), :]

    out = shape(rows, tile)
    return pl.pallas_call(
        body,
        out_shape=(out, out),
        in_specs=[pl.BlockSpec(memory_space=pltpu.VMEM)] * (len(sums) + 1),
        out_specs=(pl.BlockSpec(memory_space=pltpu.VMEM),) * 2,
        scratch_shapes=[pltpu.VMEM((count * tile, tile), F32)],
        compiler_params=pltpu.CompilerParams(vmem_limit_bytes=40 * 1024 * 1024),
    )(*sums, metric3)


def plane_place(k, rows_all):
    row = lax.axis_index("row") & 3
    if k in (1, 2):
        return row ^ jnp.where(my_kind(rows_all) == 1, 3 - k, k)
    return row ^ k


def quarter(ref, k, rows_all):
    rows = ref.shape[0] // 4
    return pl.ds(pl.multiple_of(plane_place(k, rows_all) * rows, rows), rows)


def split_halves(mine, arrived, rows_all):
    rows, width = mine.shape
    half = rows // 2

    def body(mine_ref, arrived_ref, keep_ref, send_ref):
        kind = my_kind(rows_all)
        for place, out_ref in ((kind, keep_ref), (1 - kind, send_ref)):
            here = pl.ds(pl.multiple_of(place * half, half), half)
            out_ref[...] = mine_ref[here, :] + arrived_ref[here, :]

    return call(body, (shape(half, width),) * 2, [mine, arrived], 1)


def join_quarters(parts, rows_all):
    rows, width = parts[0].shape

    def body(*refs):
        out_ref = refs[-1]
        for k in range(4):
            out_ref[quarter(out_ref, k, rows_all), :] = refs[k][...]

    return call(body, shape(4 * rows, width), parts, 1)


def add_all(parts):
    def body(*refs):
        values = [ref[...] for ref in refs[:-1]]
        while len(values) > 1:
            values = [a + b for a, b in zip(values[::2], values[1::2])]
        refs[-1][...] = values[0]

    return call(body, shape(*parts[0].shape), parts, 1)


def finish(keep, other, points, rows_all):
    rows, width = points.shape
    tile, span, upper = upper_tiles(width)

    def body(keep_ref, other_ref, points_ref, next_ref, mapped_ref, next_held, mapped_held, sems):
        odd = my_kind(rows_all) == 1
        piece = keep_ref.shape[0] // 4
        rows_of = []
        for k in range(4):
            kept, came = (ref[k * piece : (k + 1) * piece, :] for ref in (keep_ref, other_ref))
            rows_of += [jnp.where(odd, came, kept), jnp.where(odd, kept, came)]
        full = jnp.concatenate(rows_of, axis=0)
        tiles = [full[k * tile : (k + 1) * tile] for k in range(len(upper))]
        final = dict(zip(upper, tiles))
        diag = final[0, 0]
        for i in range(1, span):
            diag = diag + final[i, i]
        eye = lax.broadcasted_iota(jnp.int32, diag.shape, 0) == lax.broadcasted_iota(jnp.int32, diag.shape, 1)
        trace = jnp.sum(jnp.where(eye, diag, 0.0), keepdims=True)
        scale = width / trace
        for i, j in upper:
            value = final[i, j] * scale
            next_held[i * tile : (i + 1) * tile, j * tile : (j + 1) * tile] = value
            if i != j:
                next_held[j * tile : (j + 1) * tile, i * tile : (i + 1) * tile] = value.T
        next_copy = pltpu.make_async_copy(next_held, next_ref, sems.at[0])
        next_copy.start()
        mapped_held[...] = mul(left(points_ref[...]), right(next_held[...], axis=0))
        mapped_copy = pltpu.make_async_copy(mapped_held, mapped_ref, sems.at[1])
        mapped_copy.start()
        next_copy.wait()
        mapped_copy.wait()

    return pl.pallas_call(
        body,
        out_shape=(shape(width, width), shape(rows, width)),
        in_specs=[pl.BlockSpec(memory_space=pltpu.VMEM)] * 3,
        out_specs=(pl.BlockSpec(memory_space=pl.ANY),) * 2,
        scratch_shapes=[
            pltpu.VMEM((width, width), F32),
            pltpu.VMEM((rows, width), F32),
            pltpu.SemaphoreType.DMA((2,)),
        ],
        compiler_params=pltpu.CompilerParams(vmem_limit_bytes=40 * 1024 * 1024),
    )(keep, other, points)


def make_local(rows_all, cols_all):
    hop = make_hop(rows_all, cols_all)
    row_bits = bits_of(rows_all)
    col_bits = bits_of(cols_all)
    bit_a, bit_b = row_bits[0], row_bits[1]
    line_bits = row_bits[2:]

    def to_a(value):
        return hop(value, (bit_a, 0), (bit_b, 0))

    def to_b(value):
        return hop(value, (bit_b, 0), (bit_a, 0))

    def in_plane(parts):
        return [to_a(parts[0]), to_b(parts[1]), hop(parts[2], (bit_a | bit_b, 0))]

    def among(value, shifts):
        steps = [(0, 0)]
        for dr, dc in shifts:
            steps = steps + [(r | dr, c | dc) for r, c in steps]
        return [value] + [hop(value, step) for step in steps[1:]]

    def local(points, coeffs, metric):
        own, width = points.shape
        outs_n = coeffs.shape[1]
        points, packed = pack_own(points, coeffs)
        metric3 = metric_halves(metric)
        near = among(packed, [(bit, 0) for bit in reversed(line_bits)])
        near = near[:1] + near[:0:-1]
        across = [among(block, [(0, bit) for bit in col_bits])[1:] for block in near]
        first, late = across[0] + across[-1], [other for blocks in across[1:-1] for other in blocks]
        source = copy_after(points, first[0])
        queries = [hop(source, (bit_a | bit_b, 0)), to_a(source), to_b(source), points]
        total, mapped = early_sums(queries[:2], near + first, metric3, outs_n)
        (part_ab,) = late_sums(queries[:1], 0, total, mapped, metric3, late, outs_n)
        sent_ab = to_a(part_ab)
        (part_a,) = late_sums(queries[1:2], 1, total, mapped, metric3, late, outs_n, queries[2:3])
        sent_a = to_a(part_a)
        part_b, part_own = whole_sums(queries[2:], near + first + late, metric3, outs_n)
        half_b = part_b + sent_ab
        rest_own = to_b(half_b)
        half_own = part_own + sent_a
        rest_b = to_b(half_own)

        mine, away = outer_quarters([half_own, rest_own, half_b, rest_b], metric3, rows_all)
        keep, send = split_halves(mine, to_a(away), rows_all)
        total = add_all([keep, hop(send, (0, 1))])
        for k in range(0, len(line_bits), 2):
            total = add_all(among(total, [(bit, 0) for bit in line_bits[k : k + 2]]))
        for bit in col_bits[1:]:
            total = add_all(among(total, [(0, bit)]))
        keep = join_quarters([total] + in_plane([total] * 3), rows_all)
        return finish(keep, hop(keep, (0, 1)), points, rows_all)

    return local


def solution(mesh):
    return jax.shard_map(
        make_local(mesh.shape["row"], mesh.shape["col"]),
        mesh=mesh,
        in_specs=(P(AXES, None), P(AXES, None), P()),
        out_specs=(P(), P(AXES, None)),
        check_vma=False,
    )
```
